32 devices in a mesh: lon: 16 (over z, y, core), lat: 2 (over x).
Axes of the slice: x: 2, y: 2, z: 4, core: 2. Of those that a mesh axis runs over, the one named last changes fastest.
Arguments:
- prediction: bfloat16 [96, 384, 222], P('lat', 'lon'), may hold values from -40 to 40
- observed_state: bfloat16 [96, 384, 222], P('lat', 'lon'), may hold values from -40 to 40
- mean_state: bfloat16 [96, 384, 222], P('lat', 'lon'), may hold values from -6 to 6
- usable_point_flags: int32 [96, 384], P('lat', 'lon'), may hold values 0 or 1
- eastward_offsets: int32 [8], replicated, may hold values from 0 to 335, as said below
Outputs:
- correlation: float32 [8, 384, 222], P('lat', 'lon')
The draws below stay inside these ranges and needn't reach their ends.
Inputs may be any that keep to these rules, and one draw needn't show every extreme that they name: `eastward_offsets`: every lag lies below 336, and some lag equals 335.
All inputs are finite; a program needn't handle non-finite values. No bound on the sum of `usable_point_flags` on one device may be relied on, other than what follows from the above.
Results may differ from the reference program's by a relative error of at most 0.0044.
Values may be sent and summed in bfloat16 or wider, within the bound.
A program may use at most 64 MiB of HBM per device.

```python
import jax
import jax.numpy as jnp
from jax import lax

C = 222
K = 8
REACH = 14
LON_DEV = 24
NLAT = 96
NLON = 384


def shared_fields(key):
    split_keys = jax.random.split(jax.random.fold_in(key, 7101), 3)
    common = jax.random.normal(split_keys[0], (NLAT, NLON, C), jnp.float32)
    noise_first = jax.random.normal(split_keys[1], (NLAT, NLON, C), jnp.float32)
    noise_second = jax.random.normal(split_keys[2], (NLAT, NLON, C), jnp.float32)
    fore_values = jnp.clip(common + 0.5 * noise_first, -40.0, 40.0)
    true_values = jnp.clip(common + 0.5 * noise_second, -40.0, 40.0)
    return (fore_values, true_values)


def draw_prediction(key, part):
    return shared_fields(key)[0].astype(jnp.bfloat16)


def draw_observed_state(key, part):
    return shared_fields(key)[1].astype(jnp.bfloat16)


def draw_eastward_offsets(key, part):
    split_keys = jax.random.split(jax.random.fold_in(key, 4409), 2)
    values = jax.random.randint(split_keys[0], (K,), 0, REACH * LON_DEV, jnp.int32)
    position = jax.random.randint(split_keys[1], (), 0, K, jnp.int32)
    return values.at[position].set(REACH * LON_DEV - 1)


def with_ends(result, own_key, least, largest):
    index_at = [jax.random.randint(jax.random.fold_in(own_key, axis), (), 0, length) for axis, length in enumerate(result.shape)]
    longest = result.shape.index(max(result.shape))
    beside = index_at[:longest] + [(index_at[longest] + 1) % result.shape[longest]] + index_at[longest + 1:]
    return result.at[tuple(index_at)].set(least).at[tuple(beside)].set(largest)


def block_scale(key, shape, cuts, smallest, largest):
    def one(dim, blocks):
        steps = jax.random.uniform(jax.random.fold_in(jax.random.fold_in(key, 6), dim), (blocks,), jnp.float32, smallest / len(cuts), largest / len(cuts))
        return jnp.repeat(jnp.exp(steps), shape[dim] // blocks).reshape((-1,) + (1,) * (len(shape) - dim - 1))

    factor_of = one(*cuts[0])
    for cut in cuts[1:]:
        factor_of = factor_of * one(*cut)
    return factor_of


def scatter_about(own_key, dims, spread, bound, shards=(), held_as=jnp.bfloat16):
    entries = spread * jax.random.normal(own_key, dims, jnp.float32)
    if shards:
        entries = entries * block_scale(own_key, dims, shards, -0.22, 0.18)
    return jnp.clip(entries, -bound, bound).astype(held_as)


def setup_inputs(seed: int = 0) -> dict:
    seeds = jax.random.split(jax.random.key(seed), 6)
    prediction = draw_prediction(jax.random.fold_in(seeds[5], 71), 0)
    observed_state = draw_observed_state(jax.random.fold_in(seeds[5], 71), 0)
    mean_state = scatter_about(seeds[2], (NLAT, NLON, C), 1.0, 6.0, ((0, 2), (1, 16)))
    usable_point_flags = with_ends((jax.random.randint(seeds[3], (NLAT, NLON), 0, 5) < 4).astype(jnp.int32), jax.random.fold_in(seeds[3], 1), 0, 1)
    eastward_offsets = draw_eastward_offsets(jax.random.fold_in(seeds[5], 71), 0)
    return dict(prediction=prediction, observed_state=observed_state, mean_state=mean_state, usable_point_flags=usable_point_flags, eastward_offsets=eastward_offsets)


regular_term = 0.001

def reference(prediction, observed_state, mean_state, usable_point_flags, eastward_offsets):
    predicted_mean_state = mean_state.astype(jnp.float32)
    prediction_departure = prediction.astype(jnp.float32) - predicted_mean_state
    observed_departure = (observed_state.astype(jnp.float32) - predicted_mean_state).astype(jnp.bfloat16)
    row_index = jnp.arange(NLAT, dtype=jnp.int32).astype(jnp.float32)
    weights = jnp.cos(jnp.pi * ((row_index + 0.5) / NLAT - 0.5))
    valid_f = usable_point_flags.astype(jnp.float32)
    base_weight = weights[:, None] * valid_f
    columns = jnp.arange(NLON, dtype=jnp.int32)

    def one_lag(offset):
        source = ((columns + offset) % NLON).astype(jnp.int32)
        displaced = jnp.take(observed_departure, source, axis=1).astype(jnp.float32)
        shifted_valid = jnp.take(valid_f, source, axis=1)
        couple_factor = (base_weight * shifted_valid)[:, :, None]
        joint_moment = lax.optimization_barrier(jnp.sum(couple_factor * prediction_departure * displaced, axis=0))
        prediction_spread = lax.optimization_barrier(jnp.sum(couple_factor * prediction_departure * prediction_departure, axis=0))
        var_true = lax.optimization_barrier(jnp.sum(couple_factor * displaced * displaced, axis=0))
        return joint_moment / jnp.sqrt((prediction_spread + regular_term) * (var_true + regular_term))
    return lax.map(one_lag, eastward_offsets)
```

```python
import functools
import math

import jax
import jax.numpy as jnp
from jax import lax
from jax.experimental import pallas as pl
from jax.experimental.pallas import tpu as pltpu
from jax.sharding import PartitionSpec as P

MESH = pl.DeviceIdType.MESH
LANES = 128
SLOTS = 8
regular_term = 0.001


def exchange_kernel(n_lat, n_lon, src, dst, send_sem, recv_sem, own_sem):
    n = n_lat * n_lon
    me = lax.axis_index("lat") * n_lon + lax.axis_index("lon")

    def place(g):
        return {"lat": g // n_lon, "lon": g % n_lon}

    barrier = pltpu.get_barrier_semaphore()

    def greet(o, _):
        pl.semaphore_signal(barrier, inc=1, device_id=place((me + o) % n), device_id_type=MESH)
        return 0

    lax.fori_loop(1, n, greet, 0)
    own = pltpu.make_async_copy(src.at[me], dst.at[me], own_sem)
    own.start()
    pl.semaphore_wait(barrier, n - 1)

    def outgoing(o):
        there = (me + o) % n
        return pltpu.make_async_remote_copy(
            src_ref=src.at[there],
            dst_ref=dst.at[me],
            send_sem=send_sem.at[o],
            recv_sem=recv_sem.at[o],
            device_id=place(there),
            device_id_type=MESH,
        )

    def start(o, _):
        outgoing(o).start()
        return 0

    def finish(o, _):
        outgoing(o).wait()
        return 0

    lax.fori_loop(1, n, start, 0)
    lax.fori_loop(1, n, finish, 0)
    own.wait()


def exchange(value, n_lat, n_lon, collective_id):
    n = n_lat * n_lon
    return pl.pallas_call(
        functools.partial(exchange_kernel, n_lat, n_lon),
        out_shape=jax.ShapeDtypeStruct(value.shape, value.dtype),
        in_specs=[pl.BlockSpec(memory_space=pltpu.VMEM)],
        out_specs=pl.BlockSpec(memory_space=pltpu.VMEM),
        scratch_shapes=[
            pltpu.SemaphoreType.DMA((n,)),
            pltpu.SemaphoreType.DMA((n,)),
            pltpu.SemaphoreType.DMA,
        ],
        compiler_params=pltpu.CompilerParams(
            collective_id=collective_id, has_side_effects=True, vmem_limit_bytes=40 * 2**20
        ),
    )(value)


def lag_kernel(sizes, offsets, weights, got, out, fore_w, fore_ww, weight, truth):
    n_lat, n_lon, rows, cols, lags = sizes
    tiles = n_lon * cols // LANES
    group = math.lcm(cols, LANES) // cols
    blocks = rows // group
    width = group * cols
    per_owner = lags // n_lat
    flag = SLOTS - 1

    def unpack(step, _):
        half, block = step // blocks, step % blocks
        base = half * rows + block * group
        for d in range(n_lon):
            chunk = got[half * n_lon + d, :, pl.ds(pl.multiple_of(block * width, LANES), width)]
            chunk = chunk.astype(jnp.float32)
            for i in range(group):
                piece = chunk[:, i * cols : (i + 1) * cols]
                fore_w[base + i, :, d * cols : (d + 1) * cols] = piece[:SLOTS]
                truth[base + i, :, d * cols : (d + 1) * cols] = piece[SLOTS:]
        return 0

    lax.fori_loop(0, n_lat * blocks, unpack, 0)

    def prepare(i, _):
        w = weights[i]
        for m in range(tiles):
            at = pl.ds(m * LANES, LANES)
            fore = fore_w[i, :, at]
            usable = w * jnp.broadcast_to(fore[flag:, :], fore.shape)
            weighted = usable * fore
            weight[i, :, at] = usable
            fore_w[i, :, at] = weighted
            fore_ww[i, :, at] = weighted * fore
            true = truth[i, :, at]
            true = true * jnp.broadcast_to(true[flag:, :], true.shape)
            truth[i, :, at] = true
            if m < tiles - 1:
                truth[i, :, pl.ds((tiles + m) * LANES, LANES)] = true
        return 0

    lax.fori_loop(0, n_lat * rows, prepare, 0)

    lane = lax.broadcasted_iota(jnp.int32, (SLOTS, LANES), 1)
    zero = jnp.zeros((SLOTS, LANES), jnp.float32)
    for k in range(lags):
        first = offsets[k] // LANES
        turn = offsets[k] % LANES
        back = (LANES - turn) % LANES
        stay = lane < LANES - turn

        def row(i, totals):
            turned = [
                pltpu.roll(
                    truth[i, :, pl.ds(pl.multiple_of((first + m) * LANES, LANES), LANES)], back, 1
                )
                for m in range(tiles)
            ]
            result = []
            for m in range(tiles):
                at = pl.ds(m * LANES, LANES)
                true = jnp.where(stay, turned[m], turned[(m + 1) % tiles])
                seen = jnp.broadcast_to(true[flag:, :], true.shape)
                cov, var_fore, var_true = totals[m]
                result.append(
                    (
                        cov + fore_w[i, :, at] * true,
                        var_fore + fore_ww[i, :, at] * seen,
                        var_true + weight[i, :, at] * (true * true),
                    )
                )
            return tuple(result)

        totals = lax.fori_loop(
            0, n_lat * rows, row, tuple((zero, zero, zero) for _ in range(tiles)), unroll=4
        )
        found = jnp.concatenate(
            [
                cov / jnp.sqrt((var_fore + regular_term) * (var_true + regular_term))
                for cov, var_fore, var_true in totals
            ],
            axis=1,
        )
        owner, at = k // per_owner, k % per_owner
        for d in range(n_lon):
            out[owner * n_lon + d, :, at * cols : (at + 1) * cols] = found[
                :, d * cols : (d + 1) * cols
            ]


def by_channel(n_lat, n_lon, prediction, observed_state, mean_state, usable_point_flags, offsets):
    rows, cols, channels = prediction.shape
    lags = offsets.shape[0]
    n = n_lat * n_lon
    share = -(-channels // n)
    points = rows * cols
    total_rows, total_cols = rows * n_lat, cols * n_lon
    mean = mean_state.astype(jnp.float32)
    fore = (prediction.astype(jnp.float32) - mean).astype(jnp.bfloat16).reshape(points, channels)
    true = (observed_state.astype(jnp.float32) - mean).astype(jnp.bfloat16).reshape(points, channels)

    index = jnp.arange(n * 2 * SLOTS, dtype=jnp.int32)
    owner, slot = index // (2 * SLOTS), index % (2 * SLOTS)
    place = slot % SLOTS
    wanted = jnp.where(place < share, owner * share + place, -1)[:, None]
    hit = wanted == jnp.arange(channels, dtype=jnp.int32)[None, :]
    pick_fore = (hit & (slot < SLOTS)[:, None]).astype(jnp.bfloat16)
    pick_true = (hit & (slot >= SLOTS)[:, None]).astype(jnp.bfloat16)
    turn = functools.partial(
        lax.dot_general,
        dimension_numbers=(((1,), (1,)), ((), ())),
        preferred_element_type=jnp.float32,
    )
    packed = turn(pick_fore, fore) + turn(pick_true, true)
    flags = usable_point_flags.astype(jnp.float32).reshape(1, points)
    packed = jnp.where((place == SLOTS - 1)[:, None], flags, packed).astype(jnp.bfloat16)

    got = exchange(packed.reshape(n, 2 * SLOTS, points), n_lat, n_lon, 0)

    row_index = jnp.arange(total_rows, dtype=jnp.int32).astype(jnp.float32)
    weights = jnp.cos(jnp.pi * ((row_index + 0.5) / total_rows - 0.5))
    tiles = total_cols // LANES
    held = (total_rows, SLOTS, total_cols)
    found = pl.pallas_call(
        functools.partial(lag_kernel, (n_lat, n_lon, rows, cols, lags)),
        out_shape=jax.ShapeDtypeStruct((n, SLOTS, LANES), jnp.float32),
        in_specs=[
            pl.BlockSpec(memory_space=pltpu.SMEM),
            pl.BlockSpec(memory_space=pltpu.SMEM),
            pl.BlockSpec(memory_space=pltpu.VMEM),
        ],
        out_specs=pl.BlockSpec(memory_space=pltpu.VMEM),
        scratch_shapes=[
            pltpu.VMEM(held, jnp.float32),
            pltpu.VMEM(held, jnp.float32),
            pltpu.VMEM(held, jnp.float32),
            pltpu.VMEM((total_rows, SLOTS, (2 * tiles - 1) * LANES), jnp.float32),
        ],
        compiler_params=pltpu.CompilerParams(vmem_limit_bytes=40 * 2**20),
    )(offsets, weights, got)

    back = exchange(found, n_lat, n_lon, 1)
    mine = lags // n_lat
    back = back[:, :share, : mine * cols].reshape(n * share, mine, cols)[:channels]
    return back.transpose(1, 2, 0)


def fits(n_lat, n_lon, rows, cols, channels, lags):
    n = n_lat * n_lon
    group = math.lcm(cols, LANES) // cols
    return (
        -(-channels // n) < SLOTS
        and n <= channels
        and rows % group == 0
        and (cols * n_lon) % LANES == 0
        and lags // n_lat * cols <= LANES
    )


REACH = 14


def from_behind(value, axis, by):
    count = lax.axis_size(axis)
    return lax.ppermute(value, axis, [(i, (i + by) % count) for i in range(count)])


def ring(prediction, observed_state, mean_state, usable_point_flags, eastward_offsets):
    meridian_extent, parallel_extent, field_total = prediction.shape
    total_rows = meridian_extent * lax.axis_size("lat")
    row_index = (
        lax.axis_index("lat") * meridian_extent + jnp.arange(meridian_extent, dtype=jnp.int32)
    ).astype(jnp.float32)
    weights = jnp.cos(jnp.pi * ((row_index + 0.5) / total_rows - 0.5))
    predicted_mean_state = mean_state.astype(jnp.float32)
    prediction_departure = prediction.astype(jnp.float32) - predicted_mean_state
    observed_departure = (observed_state.astype(jnp.float32) - predicted_mean_state).astype(
        jnp.bfloat16
    )
    base_weight = weights[:, None] * usable_point_flags.astype(jnp.float32)
    window_cols = (REACH + 1) * parallel_extent
    start_true = jnp.zeros((meridian_extent, window_cols, field_total), jnp.bfloat16)
    start_true = lax.dynamic_update_slice_in_dim(start_true, observed_departure, 0, 1)
    start_valid = jnp.zeros((meridian_extent, window_cols), jnp.int32)
    start_valid = lax.dynamic_update_slice_in_dim(start_valid, usable_point_flags, 0, 1)

    def advance(turn_index, state_tuple):
        buffer_true, buffer_valid, slab_true, slab_valid = state_tuple
        slab_true, slab_valid = from_behind((slab_true, slab_valid), "lon", -1)
        place = (turn_index + 1) * parallel_extent
        buffer_true = lax.dynamic_update_slice_in_dim(buffer_true, slab_true, place, 1)
        buffer_valid = lax.dynamic_update_slice_in_dim(buffer_valid, slab_valid, place, 1)
        return (buffer_true, buffer_valid, slab_true, slab_valid)

    win_true, win_valid, unused_true, unused_valid = lax.fori_loop(
        0, REACH, advance, (start_true, start_valid, observed_departure, usable_point_flags)
    )

    def lag_sums(offset):
        frame_segment = lax.dynamic_slice_in_dim(win_true, offset, parallel_extent, 1).astype(
            jnp.float32
        )
        piece_valid = lax.dynamic_slice_in_dim(win_valid, offset, parallel_extent, 1).astype(
            jnp.float32
        )
        couple_factor = (base_weight * piece_valid)[:, :, None]
        joint_moment = jnp.sum(couple_factor * prediction_departure * frame_segment, axis=0)
        prediction_spread = jnp.sum(
            couple_factor * prediction_departure * prediction_departure, axis=0
        )
        var_true = jnp.sum(couple_factor * frame_segment * frame_segment, axis=0)
        return (joint_moment, prediction_spread, var_true)

    joint_moment, prediction_spread, var_true = lax.map(lag_sums, eastward_offsets)
    joint_moment, prediction_spread, var_true = (
        lax.psum_scatter(joint_moment, "lat", scatter_dimension=0, tiled=True),
        lax.psum_scatter(prediction_spread, "lat", scatter_dimension=0, tiled=True),
        lax.psum_scatter(var_true, "lat", scatter_dimension=0, tiled=True),
    )
    return joint_moment / jnp.sqrt((prediction_spread + regular_term) * (var_true + regular_term))


def solution(mesh):
    n_lat, n_lon = mesh.shape["lat"], mesh.shape["lon"]
    placed = (
        P("lat", "lon", None),
        P("lat", "lon", None),
        P("lat", "lon", None),
        P("lat", "lon"),
        P(),
    )

    def local(*args):
        if fits(n_lat, n_lon, *args[0].shape, args[4].shape[0]):
            return by_channel(n_lat, n_lon, *args)
        return ring(*args)

    return jax.shard_map(
        local, mesh=mesh, in_specs=placed, out_specs=P("lat", "lon", None), check_vma=False
    )
```

```python
import functools
import math

import jax
import jax.numpy as jnp
from jax import lax
from jax.experimental import pallas as pl
from jax.experimental.pallas import tpu as pltpu
from jax.sharding import PartitionSpec as P

MESH = pl.DeviceIdType.MESH
LANES = 128
SLOTS = 8
UNUSABLE = 1024.0
LIMIT = 512.0
regular_term = 0.001


def rank_of(u, n, groups):
    return ((u + 1) * n + groups - 1) // groups - 1


def lag_kernel(sizes, offsets, weights, sent, back, got, fore_w, fore_ww, weight, truth, truth_b, spread, move, total, found,
               send_sem, recv_sem, own_sem, result_sem, back_sem, last_sem):
    n_lat, n_lon, rows, cols, lags, groups = sizes
    n = n_lat * n_lon
    tiles = n_lon * cols // LANES
    group = math.lcm(cols, LANES) // cols
    phases = rows // group
    width = group * cols
    per_owner = lags // n_lat
    me = lax.axis_index("lon") * n_lat + lax.axis_index("lat")
    mine = me * groups // n
    active = (me + 1) * groups // n > mine

    def place(rank):
        return {"lat": rank % n_lat, "lon": rank // n_lat}

    def part(b):
        return pl.ds(pl.multiple_of(b * width, LANES), width)

    barrier = pltpu.get_barrier_semaphore()

    def greet(o, _):
        pl.semaphore_signal(barrier, inc=1, device_id=place((me + o) % n), device_id_type=MESH)
        return 0

    lax.fori_loop(1, n, greet, 0)

    def own(b):
        return pltpu.make_async_copy(
            sent.at[mine, :, part(b)], got.at[me, :, part(b)], own_sem.at[b]
        )

    @pl.when(active)
    def _():
        for b in range(phases):
            own(b).start()

    total[...] = jnp.zeros_like(total)
    found[...] = jnp.zeros_like(found)
    pl.semaphore_wait(barrier, n - 1)

    def outgoing(b, u):
        return pltpu.make_async_remote_copy(
            src_ref=sent.at[u, :, part(b)],
            dst_ref=got.at[me, :, part(b)],
            send_sem=send_sem.at[b, u],
            recv_sem=recv_sem.at[b, me],
            device_id=place(rank_of(u, n, groups)),
            device_id_type=MESH,
        )

    def arriving(b, rank):
        return pltpu.make_async_remote_copy(
            src_ref=got.at[rank, :, part(b)],
            dst_ref=got.at[rank, :, part(b)],
            send_sem=send_sem.at[b, 0],
            recv_sem=recv_sem.at[b, rank],
            device_id=place(rank),
            device_id_type=MESH,
        )

    for b in range(phases):

        def start(o, _, b=b):
            u = (mine + o) % groups

            @pl.when(rank_of(u, n, groups) != me)
            def _():
                outgoing(b, u).start()

            return 0

        lax.fori_loop(0, groups, start, 0)

    total_cols = n_lon * cols
    distance = lax.broadcasted_iota(jnp.int32, (total_cols, total_cols), 0) - lax.broadcasted_iota(
        jnp.int32, (total_cols, total_cols), 1
    )
    distance = jnp.where(distance < 0, distance + total_cols, distance)
    spread[...] = distance

    def build(k, _):
        move[k] = jnp.where(spread[...] == offsets[k], 1.0, 0.0).astype(jnp.bfloat16)
        return 0

    lax.fori_loop(0, lags, build, 0)
    zero = jnp.zeros((SLOTS, LANES), jnp.float32)

    def phase(b, _):
        def arrive(o, _):
            arriving(b, (me + o) % n).wait_recv()
            return 0

        own(b).wait()
        lax.fori_loop(1, n, arrive, 0)

        def unpack(half, _):
            for d in range(n_lon):
                chunk = got[d * n_lat + half, :, part(b)].astype(jnp.float32)
                for i in range(group):
                    piece = chunk[:, i * cols : (i + 1) * cols]
                    fore_w[half * group + i, :, d * cols : (d + 1) * cols] = piece[:SLOTS]
                    truth[half * group + i, :, d * cols : (d + 1) * cols] = piece[SLOTS:]
            return 0

        lax.fori_loop(0, n_lat, unpack, 0)

        def prepare(i, _):
            w = weights[i // group * rows + b * group + i % group]
            for m in range(tiles):
                at = pl.ds(m * LANES, LANES)
                fore = fore_w[i, :, at]
                usable = fore < LIMIT
                fore = jnp.where(usable, fore, 0.0)
                weighted = w * fore
                weight[i, :, at] = jnp.where(usable, w, 0.0)
                fore_w[i, :, at] = weighted
                fore_ww[i, :, at] = weighted * fore
            return 0

        lax.fori_loop(0, n_lat * group, prepare, 0, unroll=2)

        truth_b[...] = truth[...].reshape(truth_b.shape).astype(jnp.bfloat16)

        def lag(k, _):
            shifted = jnp.dot(truth_b[...], move[k], preferred_element_type=jnp.float32)
            for m in range(tiles):
                at = slice(m * LANES, (m + 1) * LANES)
                cov = var_fore = var_true = zero
                for i in range(n_lat * group):
                    true = shifted[i * SLOTS : (i + 1) * SLOTS, at]
                    seen = true < LIMIT
                    true = jnp.where(seen, true, 0.0)
                    cov += fore_w[i, :, at] * true
                    var_fore += jnp.where(seen, fore_ww[i, :, at], 0.0)
                    var_true += weight[i, :, at] * (true * true)
                total[k, 0, :, at] += cov
                total[k, 1, :, at] += var_fore
                total[k, 2, :, at] += var_true
            return 0

        lax.fori_loop(0, lags, lag, 0)
        return 0

    def returning(rank):
        return pltpu.make_async_remote_copy(
            src_ref=found.at[rank],
            dst_ref=back.at[mine],
            send_sem=result_sem.at[rank],
            recv_sem=back_sem.at[mine],
            device_id=place(rank),
            device_id_type=MESH,
        )

    def returned(u):
        return pltpu.make_async_remote_copy(
            src_ref=back.at[u],
            dst_ref=back.at[u],
            send_sem=result_sem.at[0],
            recv_sem=back_sem.at[u],
            device_id=place(rank_of(u, n, groups)),
            device_id_type=MESH,
        )

    last = pltpu.make_async_copy(found.at[me], back.at[mine], last_sem)

    @pl.when(active)
    def _():
        lax.fori_loop(0, phases, phase, 0)
        for k in range(lags):
            cov, var_fore, var_true = total[k, 0], total[k, 1], total[k, 2]
            value = cov / jnp.sqrt((var_fore + regular_term) * (var_true + regular_term))
            owner, at = k // per_owner, k % per_owner
            for d in range(n_lon):
                found[d * n_lat + owner, :, at * cols : (at + 1) * cols] = value[
                    :, d * cols : (d + 1) * cols
                ]

        def send_back(o, _):
            returning((me + o) % n).start()
            return 0

        lax.fori_loop(1, n, send_back, 0)
        last.start()

        def sent_back(o, _):
            returning((me + o) % n).wait_send()
            return 0

        lax.fori_loop(1, n, sent_back, 0)
        last.wait()

    def finish(u, _):
        @pl.when(rank_of(u, n, groups) != me)
        def _():
            for b in range(phases):
                outgoing(b, u).wait_send()
            returned(u).wait_recv()

        return 0

    lax.fori_loop(0, groups, finish, 0)


def by_channel(n_lat, n_lon, prediction, observed_state, mean_state, usable_point_flags, offsets):
    rows, cols, channels = prediction.shape
    lags = offsets.shape[0]
    n = n_lat * n_lon
    groups = -(-channels // SLOTS)
    points = rows * cols
    total_rows, total_cols = rows * n_lat, cols * n_lon
    mean = mean_state.astype(jnp.float32)
    fore = (prediction.astype(jnp.float32) - mean).astype(jnp.bfloat16).reshape(points, channels)
    true = (observed_state.astype(jnp.float32) - mean).astype(jnp.bfloat16).reshape(points, channels)

    index = jnp.arange(groups * 2 * SLOTS, dtype=jnp.int32)
    owner, slot = index // (2 * SLOTS), index % (2 * SLOTS)
    wanted = (owner * SLOTS + slot % SLOTS)[:, None]
    hit = wanted == jnp.arange(channels, dtype=jnp.int32)[None, :]
    pick_fore = (hit & (slot < SLOTS)[:, None]).astype(jnp.bfloat16)
    pick_true = (hit & (slot >= SLOTS)[:, None]).astype(jnp.bfloat16)
    turn = functools.partial(
        lax.dot_general,
        dimension_numbers=(((1,), (1,)), ((), ())),
        preferred_element_type=jnp.float32,
    )
    packed = turn(pick_fore, fore) + turn(pick_true, true)
    flags = usable_point_flags.reshape(1, points)
    packed = jnp.where(flags != 0, packed, UNUSABLE).astype(jnp.bfloat16)
    packed = packed.reshape(groups, 2 * SLOTS, points)

    row_index = jnp.arange(total_rows, dtype=jnp.int32).astype(jnp.float32)
    weights = jnp.cos(jnp.pi * ((row_index + 0.5) / total_rows - 0.5))
    group = math.lcm(cols, LANES) // cols
    phases = rows // group
    held = (n_lat * group, SLOTS, total_cols)
    back = pl.pallas_call(
        functools.partial(lag_kernel, (n_lat, n_lon, rows, cols, lags, groups)),
        out_shape=jax.ShapeDtypeStruct((groups, SLOTS, LANES), jnp.float32),
        in_specs=[
            pl.BlockSpec(memory_space=pltpu.SMEM),
            pl.BlockSpec(memory_space=pltpu.SMEM),
            pl.BlockSpec(memory_space=pltpu.VMEM),
        ],
        out_specs=pl.BlockSpec(memory_space=pltpu.VMEM),
        scratch_shapes=[
            pltpu.VMEM((n, 2 * SLOTS, points), jnp.bfloat16),
            pltpu.VMEM(held, jnp.float32),
            pltpu.VMEM(held, jnp.float32),
            pltpu.VMEM(held, jnp.float32),
            pltpu.VMEM(held, jnp.float32),
            pltpu.VMEM((n_lat * group * SLOTS, total_cols), jnp.bfloat16),
            pltpu.VMEM((total_cols, total_cols), jnp.int32),
            pltpu.VMEM((lags, total_cols, total_cols), jnp.bfloat16),
            pltpu.VMEM((lags, 3, SLOTS, total_cols), jnp.float32),
            pltpu.VMEM((n, SLOTS, LANES), jnp.float32),
            pltpu.SemaphoreType.DMA((phases, groups)),
            pltpu.SemaphoreType.DMA((phases, n)),
            pltpu.SemaphoreType.DMA((phases,)),
            pltpu.SemaphoreType.DMA((n,)),
            pltpu.SemaphoreType.DMA((groups,)),
            pltpu.SemaphoreType.DMA,
        ],
        compiler_params=pltpu.CompilerParams(
            collective_id=0, has_side_effects=True, vmem_limit_bytes=40 * 2**20
        ),
    )(offsets, weights, packed)

    mine = lags // n_lat
    back = back[:, :, : mine * cols].reshape(groups * SLOTS, mine, cols)[:channels]
    return back.transpose(1, 2, 0)


def fits(n_lat, n_lon, rows, cols, channels, lags):
    n = n_lat * n_lon
    group = math.lcm(cols, LANES) // cols
    return (
        -(-channels // SLOTS) <= n <= channels
        and rows % group == 0
        and (cols * n_lon) % LANES == 0
        and lags % n_lat == 0
        and lags // n_lat * cols <= LANES
    )


REACH = 14


def from_behind(value, axis, by):
    count = lax.axis_size(axis)
    return lax.ppermute(value, axis, [(i, (i + by) % count) for i in range(count)])


def ring(prediction, observed_state, mean_state, usable_point_flags, eastward_offsets):
    meridian_extent, parallel_extent, field_total = prediction.shape
    total_rows = meridian_extent * lax.axis_size("lat")
    row_index = (
        lax.axis_index("lat") * meridian_extent + jnp.arange(meridian_extent, dtype=jnp.int32)
    ).astype(jnp.float32)
    weights = jnp.cos(jnp.pi * ((row_index + 0.5) / total_rows - 0.5))
    predicted_mean_state = mean_state.astype(jnp.float32)
    prediction_departure = prediction.astype(jnp.float32) - predicted_mean_state
    observed_departure = (observed_state.astype(jnp.float32) - predicted_mean_state).astype(
        jnp.bfloat16
    )
    base_weight = weights[:, None] * usable_point_flags.astype(jnp.float32)
    window_cols = (REACH + 1) * parallel_extent
    start_true = jnp.zeros((meridian_extent, window_cols, field_total), jnp.bfloat16)
    start_true = lax.dynamic_update_slice_in_dim(start_true, observed_departure, 0, 1)
    start_valid = jnp.zeros((meridian_extent, window_cols), jnp.int32)
    start_valid = lax.dynamic_update_slice_in_dim(start_valid, usable_point_flags, 0, 1)

    def advance(turn_index, state_tuple):
        buffer_true, buffer_valid, slab_true, slab_valid = state_tuple
        slab_true, slab_valid = from_behind((slab_true, slab_valid), "lon", -1)
        place = (turn_index + 1) * parallel_extent
        buffer_true = lax.dynamic_update_slice_in_dim(buffer_true, slab_true, place, 1)
        buffer_valid = lax.dynamic_update_slice_in_dim(buffer_valid, slab_valid, place, 1)
        return (buffer_true, buffer_valid, slab_true, slab_valid)

    win_true, win_valid, unused_true, unused_valid = lax.fori_loop(
        0, REACH, advance, (start_true, start_valid, observed_departure, usable_point_flags)
    )

    def lag_sums(offset):
        frame_segment = lax.dynamic_slice_in_dim(win_true, offset, parallel_extent, 1).astype(
            jnp.float32
        )
        piece_valid = lax.dynamic_slice_in_dim(win_valid, offset, parallel_extent, 1).astype(
            jnp.float32
        )
        couple_factor = (base_weight * piece_valid)[:, :, None]
        joint_moment = jnp.sum(couple_factor * prediction_departure * frame_segment, axis=0)
        prediction_spread = jnp.sum(
            couple_factor * prediction_departure * prediction_departure, axis=0
        )
        var_true = jnp.sum(couple_factor * frame_segment * frame_segment, axis=0)
        return (joint_moment, prediction_spread, var_true)

    joint_moment, prediction_spread, var_true = lax.map(lag_sums, eastward_offsets)
    joint_moment, prediction_spread, var_true = (
        lax.psum_scatter(joint_moment, "lat", scatter_dimension=0, tiled=True),
        lax.psum_scatter(prediction_spread, "lat", scatter_dimension=0, tiled=True),
        lax.psum_scatter(var_true, "lat", scatter_dimension=0, tiled=True),
    )
    return joint_moment / jnp.sqrt((prediction_spread + regular_term) * (var_true + regular_term))


def solution(mesh):
    n_lat, n_lon = mesh.shape["lat"], mesh.shape["lon"]
    placed = (
        P("lat", "lon", None),
        P("lat", "lon", None),
        P("lat", "lon", None),
        P("lat", "lon"),
        P(),
    )

    def local(*args):
        if fits(n_lat, n_lon, *args[0].shape, args[4].shape[0]):
            return by_channel(n_lat, n_lon, *args)
        return ring(*args)

    return jax.shard_map(
        local, mesh=mesh, in_specs=placed, out_specs=P("lat", "lon", None), check_vma=False
    )
```

```python
import functools
import math

import jax
import jax.numpy as jnp
from jax import lax
from jax.experimental import pallas as pl
from jax.experimental.pallas import tpu as pltpu
from jax.sharding import PartitionSpec as P

MESH = pl.DeviceIdType.MESH
LANES = 128
SLOTS = 8
UNUSABLE = 1024.0
LIMIT = 512.0
regular_term = 0.001


def rank_of(u, n, groups):
    return ((u + 1) * n + groups - 1) // groups - 1


def lag_kernel(sizes, offsets, weights, sent, back, got, fore_w, fore_ww, weight, truth, total, found,
               send_sem, recv_sem, own_sem, result_sem, back_sem, last_sem):
    n_lat, n_lon, rows, cols, lags, groups = sizes
    n = n_lat * n_lon
    tiles = n_lon * cols // LANES
    group = math.lcm(cols, LANES) // cols
    phases = rows // group
    width = group * cols
    per_owner = lags // n_lat
    me = lax.axis_index("lon") * n_lat + lax.axis_index("lat")
    mine = me * groups // n
    active = (me + 1) * groups // n > mine

    def place(rank):
        return {"lat": rank % n_lat, "lon": rank // n_lat}

    def part(b):
        return pl.ds(pl.multiple_of(b * width, LANES), width)

    barrier = pltpu.get_barrier_semaphore()

    def greet(o, _):
        pl.semaphore_signal(barrier, inc=1, device_id=place((me + o) % n), device_id_type=MESH)
        return 0

    lax.fori_loop(1, n, greet, 0)

    def own(b):
        return pltpu.make_async_copy(
            sent.at[mine, :, part(b)], got.at[me, :, part(b)], own_sem.at[b]
        )

    @pl.when(active)
    def _():
        for b in range(phases):
            own(b).start()

    total[...] = jnp.zeros_like(total)
    found[...] = jnp.zeros_like(found)
    pl.semaphore_wait(barrier, n - 1)

    def outgoing(b, u):
        return pltpu.make_async_remote_copy(
            src_ref=sent.at[u, :, part(b)],
            dst_ref=got.at[me, :, part(b)],
            send_sem=send_sem.at[b, u],
            recv_sem=recv_sem.at[b, me],
            device_id=place(rank_of(u, n, groups)),
            device_id_type=MESH,
        )

    def arriving(b, rank):
        return pltpu.make_async_remote_copy(
            src_ref=got.at[rank, :, part(b)],
            dst_ref=got.at[rank, :, part(b)],
            send_sem=send_sem.at[b, 0],
            recv_sem=recv_sem.at[b, rank],
            device_id=place(rank),
            device_id_type=MESH,
        )

    for b in range(phases):

        def start(o, _, b=b):
            u = (mine + o // 2 + o % 2 * ((groups + 1) // 2)) % groups

            @pl.when(rank_of(u, n, groups) != me)
            def _():
                outgoing(b, u).start()

            return 0

        lax.fori_loop(0, groups, start, 0)

    lane = lax.broadcasted_iota(jnp.int32, (SLOTS, LANES), 1)
    zero = jnp.zeros((SLOTS, LANES), jnp.float32)

    def phase(b, _):
        def arrive(o, _):
            arriving(b, (me + o) % n).wait_recv()
            return 0

        own(b).wait()
        lax.fori_loop(1, n, arrive, 0)

        def unpack(half, _):
            for d in range(n_lon):
                chunk = got[d * n_lat + half, :, part(b)].astype(jnp.float32)
                for i in range(group):
                    piece = chunk[:, i * cols : (i + 1) * cols]
                    fore_w[half * group + i, :, d * cols : (d + 1) * cols] = piece[:SLOTS]
                    truth[half * group + i, :, d * cols : (d + 1) * cols] = piece[SLOTS:]
            return 0

        lax.fori_loop(0, n_lat, unpack, 0)

        def prepare(i, _):
            w = weights[i // group * rows + b * group + i % group]
            for m in range(tiles):
                at = pl.ds(m * LANES, LANES)
                fore = fore_w[i, :, at]
                usable = fore < LIMIT
                fore = jnp.where(usable, fore, 0.0)
                weighted = w * fore
                weight[i, :, at] = jnp.where(usable, w, 0.0)
                fore_w[i, :, at] = weighted
                fore_ww[i, :, at] = weighted * fore
            return 0

        lax.fori_loop(0, n_lat * group, prepare, 0, unroll=2)

        def lag(k, _):
            shift = offsets[k]
            first, turn = lax.div(shift, LANES), lax.rem(shift, LANES)
            stay = lane < LANES - turn
            sums = [(zero, zero, zero)] * tiles
            for i in range(n_lat * group):
                turned = [
                    pltpu.roll(truth[i, :, m * LANES : (m + 1) * LANES], LANES - turn, 1)
                    for m in range(tiles)
                ]
                ahead = []
                for m in range(tiles):
                    value = turned[m]
                    for f in range(1, tiles):
                        value = jnp.where(first == f, turned[(m + f) % tiles], value)
                    ahead.append(value)
                for m in range(tiles):
                    at = slice(m * LANES, (m + 1) * LANES)
                    true = jnp.where(stay, ahead[m], ahead[(m + 1) % tiles])
                    seen = true < LIMIT
                    true = jnp.where(seen, true, 0.0)
                    cov, var_fore, var_true = sums[m]
                    sums[m] = (
                        cov + fore_w[i, :, at] * true,
                        var_fore + jnp.where(seen, fore_ww[i, :, at], 0.0),
                        var_true + weight[i, :, at] * (true * true),
                    )
            for m in range(tiles):
                at = slice(m * LANES, (m + 1) * LANES)
                for q in range(3):
                    total[k, q, :, at] += sums[m][q]
            return 0

        lax.fori_loop(0, lags, lag, 0)
        return 0

    def returning(rank):
        return pltpu.make_async_remote_copy(
            src_ref=found.at[rank],
            dst_ref=back.at[mine],
            send_sem=result_sem.at[rank],
            recv_sem=back_sem.at[mine],
            device_id=place(rank),
            device_id_type=MESH,
        )

    def returned(u):
        return pltpu.make_async_remote_copy(
            src_ref=back.at[u],
            dst_ref=back.at[u],
            send_sem=result_sem.at[0],
            recv_sem=back_sem.at[u],
            device_id=place(rank_of(u, n, groups)),
            device_id_type=MESH,
        )

    last = pltpu.make_async_copy(found.at[me], back.at[mine], last_sem)

    @pl.when(active)
    def _():
        lax.fori_loop(0, phases, phase, 0)
        for k in range(lags):
            cov, var_fore, var_true = total[k, 0], total[k, 1], total[k, 2]
            value = cov / jnp.sqrt((var_fore + regular_term) * (var_true + regular_term))
            owner, at = k // per_owner, k % per_owner
            for d in range(n_lon):
                found[d * n_lat + owner, :, at * cols : (at + 1) * cols] = value[
                    :, d * cols : (d + 1) * cols
                ]

        def send_back(o, _):
            returning((me + o) % n).start()
            return 0

        lax.fori_loop(1, n, send_back, 0)
        last.start()

        def sent_back(o, _):
            returning((me + o) % n).wait_send()
            return 0

        lax.fori_loop(1, n, sent_back, 0)
        last.wait()

    def finish(u, _):
        @pl.when(rank_of(u, n, groups) != me)
        def _():
            for b in range(phases):
                outgoing(b, u).wait_send()
            returned(u).wait_recv()

        return 0

    lax.fori_loop(0, groups, finish, 0)


def by_channel(n_lat, n_lon, prediction, observed_state, mean_state, usable_point_flags, offsets):
    rows, cols, channels = prediction.shape
    lags = offsets.shape[0]
    n = n_lat * n_lon
    groups = -(-channels // SLOTS)
    points = rows * cols
    total_rows, total_cols = rows * n_lat, cols * n_lon
    mean = mean_state.astype(jnp.float32)
    fore = (prediction.astype(jnp.float32) - mean).astype(jnp.bfloat16).reshape(points, channels)
    true = (observed_state.astype(jnp.float32) - mean).astype(jnp.bfloat16).reshape(points, channels)

    index = jnp.arange(groups * 2 * SLOTS, dtype=jnp.int32)
    owner, slot = index // (2 * SLOTS), index % (2 * SLOTS)
    wanted = (owner * SLOTS + slot % SLOTS)[:, None]
    hit = wanted == jnp.arange(channels, dtype=jnp.int32)[None, :]
    pick_fore = (hit & (slot < SLOTS)[:, None]).astype(jnp.bfloat16)
    pick_true = (hit & (slot >= SLOTS)[:, None]).astype(jnp.bfloat16)
    turn = functools.partial(
        lax.dot_general,
        dimension_numbers=(((1,), (1,)), ((), ())),
        preferred_element_type=jnp.float32,
    )
    packed = turn(pick_fore, fore) + turn(pick_true, true)
    flags = usable_point_flags.reshape(1, points)
    packed = jnp.where(flags != 0, packed, UNUSABLE).astype(jnp.bfloat16)
    packed = packed.reshape(groups, 2 * SLOTS, points)

    row_index = jnp.arange(total_rows, dtype=jnp.int32).astype(jnp.float32)
    weights = jnp.cos(jnp.pi * ((row_index + 0.5) / total_rows - 0.5))
    group = math.lcm(cols, LANES) // cols
    phases = rows // group
    held = (n_lat * group, SLOTS, total_cols)
    back = pl.pallas_call(
        functools.partial(lag_kernel, (n_lat, n_lon, rows, cols, lags, groups)),
        out_shape=jax.ShapeDtypeStruct((groups, SLOTS, LANES), jnp.float32),
        in_specs=[
            pl.BlockSpec(memory_space=pltpu.SMEM),
            pl.BlockSpec(memory_space=pltpu.SMEM),
            pl.BlockSpec(memory_space=pltpu.VMEM),
        ],
        out_specs=pl.BlockSpec(memory_space=pltpu.VMEM),
        scratch_shapes=[
            pltpu.VMEM((n, 2 * SLOTS, points), jnp.bfloat16),
            pltpu.VMEM(held, jnp.float32),
            pltpu.VMEM(held, jnp.float32),
            pltpu.VMEM(held, jnp.float32),
            pltpu.VMEM(held, jnp.float32),
            pltpu.VMEM((lags, 3, SLOTS, total_cols), jnp.float32),
            pltpu.VMEM((n, SLOTS, LANES), jnp.float32),
            pltpu.SemaphoreType.DMA((phases, groups)),
            pltpu.SemaphoreType.DMA((phases, n)),
            pltpu.SemaphoreType.DMA((phases,)),
            pltpu.SemaphoreType.DMA((n,)),
            pltpu.SemaphoreType.DMA((groups,)),
            pltpu.SemaphoreType.DMA,
        ],
        compiler_params=pltpu.CompilerParams(
            collective_id=0, has_side_effects=True, vmem_limit_bytes=40 * 2**20
        ),
    )(offsets, weights, packed)

    mine = lags // n_lat
    back = back[:, :, : mine * cols].reshape(groups * SLOTS, mine, cols)[:channels]
    return back.transpose(1, 2, 0)


def fits(n_lat, n_lon, rows, cols, channels, lags):
    n = n_lat * n_lon
    group = math.lcm(cols, LANES) // cols
    return (
        -(-channels // SLOTS) <= n <= channels
        and rows % group == 0
        and (cols * n_lon) % LANES == 0
        and lags % n_lat == 0
        and lags // n_lat * cols <= LANES
    )


REACH = 14


def from_behind(value, axis, by):
    count = lax.axis_size(axis)
    return lax.ppermute(value, axis, [(i, (i + by) % count) for i in range(count)])


def ring(prediction, observed_state, mean_state, usable_point_flags, eastward_offsets):
    meridian_extent, parallel_extent, field_total = prediction.shape
    total_rows = meridian_extent * lax.axis_size("lat")
    row_index = (
        lax.axis_index("lat") * meridian_extent + jnp.arange(meridian_extent, dtype=jnp.int32)
    ).astype(jnp.float32)
    weights = jnp.cos(jnp.pi * ((row_index + 0.5) / total_rows - 0.5))
    predicted_mean_state = mean_state.astype(jnp.float32)
    prediction_departure = prediction.astype(jnp.float32) - predicted_mean_state
    observed_departure = (observed_state.astype(jnp.float32) - predicted_mean_state).astype(
        jnp.bfloat16
    )
    base_weight = weights[:, None] * usable_point_flags.astype(jnp.float32)
    window_cols = (REACH + 1) * parallel_extent
    start_true = jnp.zeros((meridian_extent, window_cols, field_total), jnp.bfloat16)
    start_true = lax.dynamic_update_slice_in_dim(start_true, observed_departure, 0, 1)
    start_valid = jnp.zeros((meridian_extent, window_cols), jnp.int32)
    start_valid = lax.dynamic_update_slice_in_dim(start_valid, usable_point_flags, 0, 1)

    def advance(turn_index, state_tuple):
        buffer_true, buffer_valid, slab_true, slab_valid = state_tuple
        slab_true, slab_valid = from_behind((slab_true, slab_valid), "lon", -1)
        place = (turn_index + 1) * parallel_extent
        buffer_true = lax.dynamic_update_slice_in_dim(buffer_true, slab_true, place, 1)
        buffer_valid = lax.dynamic_update_slice_in_dim(buffer_valid, slab_valid, place, 1)
        return (buffer_true, buffer_valid, slab_true, slab_valid)

    win_true, win_valid, unused_true, unused_valid = lax.fori_loop(
        0, REACH, advance, (start_true, start_valid, observed_departure, usable_point_flags)
    )

    def lag_sums(offset):
        frame_segment = lax.dynamic_slice_in_dim(win_true, offset, parallel_extent, 1).astype(
            jnp.float32
        )
        piece_valid = lax.dynamic_slice_in_dim(win_valid, offset, parallel_extent, 1).astype(
            jnp.float32
        )
        couple_factor = (base_weight * piece_valid)[:, :, None]
        joint_moment = jnp.sum(couple_factor * prediction_departure * frame_segment, axis=0)
        prediction_spread = jnp.sum(
            couple_factor * prediction_departure * prediction_departure, axis=0
        )
        var_true = jnp.sum(couple_factor * frame_segment * frame_segment, axis=0)
        return (joint_moment, prediction_spread, var_true)

    joint_moment, prediction_spread, var_true = lax.map(lag_sums, eastward_offsets)
    joint_moment, prediction_spread, var_true = (
        lax.psum_scatter(joint_moment, "lat", scatter_dimension=0, tiled=True),
        lax.psum_scatter(prediction_spread, "lat", scatter_dimension=0, tiled=True),
        lax.psum_scatter(var_true, "lat", scatter_dimension=0, tiled=True),
    )
    return joint_moment / jnp.sqrt((prediction_spread + regular_term) * (var_true + regular_term))


def solution(mesh):
    n_lat, n_lon = mesh.shape["lat"], mesh.shape["lon"]
    placed = (
        P("lat", "lon", None),
        P("lat", "lon", None),
        P("lat", "lon", None),
        P("lat", "lon"),
        P(),
    )

    def local(*args):
        if fits(n_lat, n_lon, *args[0].shape, args[4].shape[0]):
            return by_channel(n_lat, n_lon, *args)
        return ring(*args)

    return jax.shard_map(
        local, mesh=mesh, in_specs=placed, out_specs=P("lat", "lon", None), check_vma=False
    )
```

```python
import functools
import math

import jax
import jax.numpy as jnp
from jax import lax
from jax.experimental import pallas as pl
from jax.experimental.pallas import tpu as pltpu
from jax.sharding import PartitionSpec as P

MESH = pl.DeviceIdType.MESH
LANES = 128
SLOTS = 8
UNUSABLE = 1024.0
LIMIT = 512.0
regular_term = 0.001


def rank_of(u, n, groups):
    return ((u + 1) * n + groups - 1) // groups - 1


def lag_kernel(sizes, offsets, weights, flags, prediction, observed, mean, out,
               fields, sent, back, got, fore_w, fore_ww, weight, truth, total, found,
               load_sem, send_sem, recv_sem, own_sem, result_sem, back_sem, last_sem):
    n_lat, n_lon, rows, cols, lags, groups = sizes
    n = n_lat * n_lon
    tiles = n_lon * cols // LANES
    group = math.lcm(cols, LANES) // cols
    phases = rows // group
    width = group * cols
    per_owner = lags // n_lat
    me = lax.axis_index("lon") * n_lat + lax.axis_index("lat")
    mine = me * groups // n
    active = (me + 1) * groups // n > mine

    def place(rank):
        return {"lat": rank % n_lat, "lon": rank // n_lat}

    def part(b):
        return pl.ds(pl.multiple_of(b * width, LANES), width)

    barrier = pltpu.get_barrier_semaphore()

    def greet(o, _):
        pl.semaphore_signal(barrier, inc=1, device_id=place((me + o) % n), device_id_type=MESH)
        return 0

    lax.fori_loop(1, n, greet, 0)

    def load(b):
        at = pl.ds(b * group, group)
        return [
            pltpu.make_async_copy(source.at[at], fields.at[q, at], load_sem.at[q, b])
            for q, source in enumerate((prediction, observed, mean))
        ]

    for b in range(phases):
        for copy in load(b):
            copy.start()

    channels = prediction.shape[2]
    identity = jnp.where(
        lax.broadcasted_iota(jnp.int32, (groups * SLOTS, channels), 0)
        == lax.broadcasted_iota(jnp.int32, (groups * SLOTS, channels), 1),
        1.0,
        0.0,
    ).astype(jnp.bfloat16)

    def pack(b):
        for copy in load(b):
            copy.wait()
        fore, true = [], []
        for i in range(b * group, (b + 1) * group):
            usable = jnp.broadcast_to(flags[:, i : i + 1], (cols, channels)) != 0
            middle = fields[2, i].astype(jnp.float32)
            fore.append(jnp.where(usable, fields[0, i].astype(jnp.float32) - middle, UNUSABLE))
            true.append(jnp.where(usable, fields[1, i].astype(jnp.float32) - middle, UNUSABLE))
        turned = [
            lax.dot_general(
                identity,
                jnp.concatenate(values, axis=0).astype(jnp.bfloat16),
                (((1,), (1,)), ((), ())),
                preferred_element_type=jnp.float32,
            ).reshape(groups, SLOTS, width)
            for values in (fore, true)
        ]
        sent[:, :, b * width : (b + 1) * width] = jnp.concatenate(turned, axis=1).astype(
            jnp.bfloat16
        )

    def own(b):
        return pltpu.make_async_copy(
            sent.at[mine, :, part(b)], got.at[me, :, part(b)], own_sem.at[b]
        )

    pack(0)
    total[...] = jnp.zeros_like(total)
    found[...] = jnp.zeros_like(found)
    pl.semaphore_wait(barrier, n - 1)

    def outgoing(b, u):
        return pltpu.make_async_remote_copy(
            src_ref=sent.at[u, :, part(b)],
            dst_ref=got.at[me, :, part(b)],
            send_sem=send_sem.at[b, u],
            recv_sem=recv_sem.at[b, me],
            device_id=place(rank_of(u, n, groups)),
            device_id_type=MESH,
        )

    def arriving(b, rank):
        return pltpu.make_async_remote_copy(
            src_ref=got.at[rank, :, part(b)],
            dst_ref=got.at[rank, :, part(b)],
            send_sem=send_sem.at[b, 0],
            recv_sem=recv_sem.at[b, rank],
            device_id=place(rank),
            device_id_type=MESH,
        )

    for b in range(phases):
        if b > 0:
            pack(b)

        @pl.when(active)
        def _(b=b):
            own(b).start()

        def start(o, _, b=b):
            u = (mine + o // 2 + o % 2 * ((groups + 1) // 2)) % groups

            @pl.when(rank_of(u, n, groups) != me)
            def _():
                outgoing(b, u).start()

            return 0

        lax.fori_loop(0, groups, start, 0)

    lane = lax.broadcasted_iota(jnp.int32, (SLOTS, LANES), 1)
    zero = jnp.zeros((SLOTS, LANES), jnp.float32)

    def phase(b, _):
        def arrive(o, _):
            arriving(b, (me + o) % n).wait_recv()
            return 0

        own(b).wait()
        lax.fori_loop(1, n, arrive, 0)

        def unpack(half, _):
            for d in range(n_lon):
                chunk = got[d * n_lat + half, :, part(b)].astype(jnp.float32)
                for i in range(group):
                    piece = chunk[:, i * cols : (i + 1) * cols]
                    fore_w[half * group + i, :, d * cols : (d + 1) * cols] = piece[:SLOTS]
                    truth[half * group + i, :, d * cols : (d + 1) * cols] = piece[SLOTS:]
            return 0

        lax.fori_loop(0, n_lat, unpack, 0)

        def prepare(i, _):
            w = weights[i // group * rows + b * group + i % group]
            for m in range(tiles):
                at = pl.ds(m * LANES, LANES)
                fore = fore_w[i, :, at]
                usable = fore < LIMIT
                fore = jnp.where(usable, fore, 0.0)
                weighted = w * fore
                weight[i, :, at] = jnp.where(usable, w, 0.0)
                fore_w[i, :, at] = weighted
                fore_ww[i, :, at] = weighted * fore
            return 0

        lax.fori_loop(0, n_lat * group, prepare, 0, unroll=2)

        def lag(k, _):
            shift = offsets[k]
            first, turn = lax.div(shift, LANES), lax.rem(shift, LANES)
            stay = lane < LANES - turn
            back_turn = lax.rem(LANES - turn, LANES)
            sums = [(zero, zero, zero)] * tiles
            for i in range(n_lat * group):
                turned = [
                    pltpu.roll(truth[i, :, m * LANES : (m + 1) * LANES], back_turn, 1)
                    for m in range(tiles)
                ]
                ahead = []
                for m in range(tiles):
                    value = turned[m]
                    for f in range(1, tiles):
                        value = jnp.where(first == f, turned[(m + f) % tiles], value)
                    ahead.append(value)
                for m in range(tiles):
                    at = slice(m * LANES, (m + 1) * LANES)
                    true = jnp.where(stay, ahead[m], ahead[(m + 1) % tiles])
                    seen = true < LIMIT
                    true = jnp.where(seen, true, 0.0)
                    cov, var_fore, var_true = sums[m]
                    sums[m] = (
                        cov + fore_w[i, :, at] * true,
                        var_fore + jnp.where(seen, fore_ww[i, :, at], 0.0),
                        var_true + weight[i, :, at] * (true * true),
                    )
            for m in range(tiles):
                at = slice(m * LANES, (m + 1) * LANES)
                for q in range(3):
                    total[k, q, :, at] += sums[m][q]
            return 0

        lax.fori_loop(0, lags, lag, 0)
        return 0

    def returning(rank):
        return pltpu.make_async_remote_copy(
            src_ref=found.at[rank],
            dst_ref=back.at[mine],
            send_sem=result_sem.at[rank],
            recv_sem=back_sem.at[mine],
            device_id=place(rank),
            device_id_type=MESH,
        )

    def returned(u):
        return pltpu.make_async_remote_copy(
            src_ref=back.at[u],
            dst_ref=back.at[u],
            send_sem=result_sem.at[0],
            recv_sem=back_sem.at[u],
            device_id=place(rank_of(u, n, groups)),
            device_id_type=MESH,
        )

    last = pltpu.make_async_copy(found.at[me], back.at[mine], last_sem)

    @pl.when(active)
    def _():
        lax.fori_loop(0, phases, phase, 0)
        for k in range(lags):
            cov, var_fore, var_true = total[k, 0], total[k, 1], total[k, 2]
            value = cov / jnp.sqrt((var_fore + regular_term) * (var_true + regular_term))
            owner, at = k // per_owner, k % per_owner
            for d in range(n_lon):
                found[d * n_lat + owner, :, at * cols : (at + 1) * cols] = value[
                    :, d * cols : (d + 1) * cols
                ]

        def send_back(o, _):
            returning((me + o) % n).start()
            return 0

        lax.fori_loop(1, n, send_back, 0)
        last.start()

        def sent_back(o, _):
            returning((me + o) % n).wait_send()
            return 0

        lax.fori_loop(1, n, sent_back, 0)

    def finish(u, _):
        @pl.when(rank_of(u, n, groups) != me)
        def _():
            for b in range(phases):
                outgoing(b, u).wait_send()
            returned(u).wait_recv()

        return 0

    lax.fori_loop(0, groups, finish, 0)

    @pl.when(active)
    def _():
        last.wait()

    correlation = back[...].reshape(groups * SLOTS, LANES).T
    out[...] = correlation[: per_owner * cols, :channels]


def by_channel(n_lat, n_lon, prediction, observed_state, mean_state, usable_point_flags, offsets):
    rows, cols, channels = prediction.shape
    lags = offsets.shape[0]
    n = n_lat * n_lon
    groups = -(-channels // SLOTS)
    points = rows * cols
    total_rows, total_cols = rows * n_lat, cols * n_lon
    row_index = jnp.arange(total_rows, dtype=jnp.int32).astype(jnp.float32)
    weights = jnp.cos(jnp.pi * ((row_index + 0.5) / total_rows - 0.5))
    group = math.lcm(cols, LANES) // cols
    phases = rows // group
    held = (n_lat * group, SLOTS, total_cols)
    mine = lags // n_lat
    found = pl.pallas_call(
        functools.partial(lag_kernel, (n_lat, n_lon, rows, cols, lags, groups)),
        out_shape=jax.ShapeDtypeStruct((mine * cols, channels), jnp.float32),
        in_specs=[
            pl.BlockSpec(memory_space=pltpu.SMEM),
            pl.BlockSpec(memory_space=pltpu.SMEM),
            pl.BlockSpec(memory_space=pltpu.VMEM),
            pl.BlockSpec(memory_space=pl.ANY),
            pl.BlockSpec(memory_space=pl.ANY),
            pl.BlockSpec(memory_space=pl.ANY),
        ],
        out_specs=pl.BlockSpec(memory_space=pltpu.VMEM),
        scratch_shapes=[
            pltpu.VMEM((3, rows, cols, channels), jnp.bfloat16),
            pltpu.VMEM((groups, 2 * SLOTS, points), jnp.bfloat16),
            pltpu.VMEM((groups, SLOTS, LANES), jnp.float32),
            pltpu.VMEM((n, 2 * SLOTS, points), jnp.bfloat16),
            pltpu.VMEM(held, jnp.float32),
            pltpu.VMEM(held, jnp.float32),
            pltpu.VMEM(held, jnp.float32),
            pltpu.VMEM(held, jnp.float32),
            pltpu.VMEM((lags, 3, SLOTS, total_cols), jnp.float32),
            pltpu.VMEM((n, SLOTS, LANES), jnp.float32),
            pltpu.SemaphoreType.DMA((3, phases)),
            pltpu.SemaphoreType.DMA((phases, groups)),
            pltpu.SemaphoreType.DMA((phases, n)),
            pltpu.SemaphoreType.DMA((phases,)),
            pltpu.SemaphoreType.DMA((n,)),
            pltpu.SemaphoreType.DMA((groups,)),
            pltpu.SemaphoreType.DMA,
        ],
        compiler_params=pltpu.CompilerParams(
            collective_id=0, has_side_effects=True, vmem_limit_bytes=60 * 2**20
        ),
    )(offsets, weights, usable_point_flags.T, prediction, observed_state, mean_state)
    return found.reshape(mine, cols, channels)


def fits(n_lat, n_lon, rows, cols, channels, lags):
    n = n_lat * n_lon
    group = math.lcm(cols, LANES) // cols
    return (
        -(-channels // SLOTS) <= n <= channels
        and cols % SLOTS == 0
        and rows % group == 0
        and (cols * n_lon) % LANES == 0
        and lags % n_lat == 0
        and lags // n_lat * cols <= LANES
    )


REACH = 14


def from_behind(value, axis, by):
    count = lax.axis_size(axis)
    return lax.ppermute(value, axis, [(i, (i + by) % count) for i in range(count)])


def ring(prediction, observed_state, mean_state, usable_point_flags, eastward_offsets):
    meridian_extent, parallel_extent, field_total = prediction.shape
    total_rows = meridian_extent * lax.axis_size("lat")
    row_index = (
        lax.axis_index("lat") * meridian_extent + jnp.arange(meridian_extent, dtype=jnp.int32)
    ).astype(jnp.float32)
    weights = jnp.cos(jnp.pi * ((row_index + 0.5) / total_rows - 0.5))
    predicted_mean_state = mean_state.astype(jnp.float32)
    prediction_departure = prediction.astype(jnp.float32) - predicted_mean_state
    observed_departure = (observed_state.astype(jnp.float32) - predicted_mean_state).astype(
        jnp.bfloat16
    )
    base_weight = weights[:, None] * usable_point_flags.astype(jnp.float32)
    window_cols = (REACH + 1) * parallel_extent
    start_true = jnp.zeros((meridian_extent, window_cols, field_total), jnp.bfloat16)
    start_true = lax.dynamic_update_slice_in_dim(start_true, observed_departure, 0, 1)
    start_valid = jnp.zeros((meridian_extent, window_cols), jnp.int32)
    start_valid = lax.dynamic_update_slice_in_dim(start_valid, usable_point_flags, 0, 1)

    def advance(turn_index, state_tuple):
        buffer_true, buffer_valid, slab_true, slab_valid = state_tuple
        slab_true, slab_valid = from_behind((slab_true, slab_valid), "lon", -1)
        place = (turn_index + 1) * parallel_extent
        buffer_true = lax.dynamic_update_slice_in_dim(buffer_true, slab_true, place, 1)
        buffer_valid = lax.dynamic_update_slice_in_dim(buffer_valid, slab_valid, place, 1)
        return (buffer_true, buffer_valid, slab_true, slab_valid)

    win_true, win_valid, unused_true, unused_valid = lax.fori_loop(
        0, REACH, advance, (start_true, start_valid, observed_departure, usable_point_flags)
    )

    def lag_sums(offset):
        frame_segment = lax.dynamic_slice_in_dim(win_true, offset, parallel_extent, 1).astype(
            jnp.float32
        )
        piece_valid = lax.dynamic_slice_in_dim(win_valid, offset, parallel_extent, 1).astype(
            jnp.float32
        )
        couple_factor = (base_weight * piece_valid)[:, :, None]
        joint_moment = jnp.sum(couple_factor * prediction_departure * frame_segment, axis=0)
        prediction_spread = jnp.sum(
            couple_factor * prediction_departure * prediction_departure, axis=0
        )
        var_true = jnp.sum(couple_factor * frame_segment * frame_segment, axis=0)
        return (joint_moment, prediction_spread, var_true)

    joint_moment, prediction_spread, var_true = lax.map(lag_sums, eastward_offsets)
    joint_moment, prediction_spread, var_true = (
        lax.psum_scatter(joint_moment, "lat", scatter_dimension=0, tiled=True),
        lax.psum_scatter(prediction_spread, "lat", scatter_dimension=0, tiled=True),
        lax.psum_scatter(var_true, "lat", scatter_dimension=0, tiled=True),
    )
    return joint_moment / jnp.sqrt((prediction_spread + regular_term) * (var_true + regular_term))


def solution(mesh):
    n_lat, n_lon = mesh.shape["lat"], mesh.shape["lon"]
    placed = (
        P("lat", "lon", None),
        P("lat", "lon", None),
        P("lat", "lon", None),
        P("lat", "lon"),
        P(),
    )

    def local(*args):
        if fits(n_lat, n_lon, *args[0].shape, args[4].shape[0]):
            return by_channel(n_lat, n_lon, *args)
        return ring(*args)

    return jax.shard_map(
        local, mesh=mesh, in_specs=placed, out_specs=P("lat", "lon", None), check_vma=False
    )
```

```python
import functools
import math

import jax
import jax.numpy as jnp
from jax import lax
from jax.experimental import pallas as pl
from jax.experimental.pallas import tpu as pltpu
from jax.sharding import PartitionSpec as P

MESH = pl.DeviceIdType.MESH
LANES = 128
SLOTS = 8
UNUSABLE = 1024.0
LIMIT = 512.0
regular_term = 0.001


def rank_of(u, n, groups):
    return ((u + 1) * n + groups - 1) // groups - 1


def lag_kernel(sizes, offsets, weights, flags, prediction, observed, mean, out,
               fields, sent, back, got, both, fore_w, fore_ww, weight, truth, total, found,
               load_sem, send_sem, recv_sem, own_sem, result_sem, back_sem, last_sem):
    n_lat, n_lon, rows, cols, lags, groups = sizes
    n = n_lat * n_lon
    tiles = n_lon * cols // LANES
    group = math.lcm(cols, LANES) // cols
    phases = rows // group
    width = group * cols
    per_owner = lags // n_lat
    me = lax.axis_index("lon") * n_lat + lax.axis_index("lat")
    mine = me * groups // n
    active = (me + 1) * groups // n > mine

    def place(rank):
        return {"lat": rank % n_lat, "lon": rank // n_lat}

    def part(b):
        return pl.ds(pl.multiple_of(b * width, LANES), width)

    barrier = pltpu.get_barrier_semaphore()

    def greet(o, _):
        pl.semaphore_signal(barrier, inc=1, device_id=place((me + o) % n), device_id_type=MESH)
        return 0

    lax.fori_loop(1, n, greet, 0)

    def load(b):
        at = pl.ds(b * group, group)
        return [
            pltpu.make_async_copy(source.at[at], fields.at[q, at], load_sem.at[q, b])
            for q, source in enumerate((prediction, observed, mean))
        ]

    for b in range(phases):
        for copy in load(b):
            copy.start()

    channels = prediction.shape[2]
    identity = jnp.where(
        lax.broadcasted_iota(jnp.int32, (groups * SLOTS, channels), 0)
        == lax.broadcasted_iota(jnp.int32, (groups * SLOTS, channels), 1),
        1.0,
        0.0,
    ).astype(jnp.bfloat16)

    def pack(b):
        for copy in load(b):
            copy.wait()
        fore, true = [], []
        for i in range(b * group, (b + 1) * group):
            usable = jnp.broadcast_to(flags[:, i : i + 1], (cols, channels)) != 0
            middle = fields[2, i].astype(jnp.float32)
            fore.append(jnp.where(usable, fields[0, i].astype(jnp.float32) - middle, UNUSABLE))
            true.append(jnp.where(usable, fields[1, i].astype(jnp.float32) - middle, UNUSABLE))
        turned = [
            lax.dot_general(
                identity,
                jnp.concatenate(values, axis=0).astype(jnp.bfloat16),
                (((1,), (1,)), ((), ())),
                preferred_element_type=jnp.float32,
            ).reshape(groups, SLOTS, width)
            for values in (fore, true)
        ]
        sent[:, :, b * width : (b + 1) * width] = jnp.concatenate(turned, axis=1).astype(
            jnp.bfloat16
        )

    def own(b):
        return pltpu.make_async_copy(
            sent.at[mine, :, part(b)], got.at[me, :, part(b)], own_sem.at[b]
        )

    pack(0)
    total[...] = jnp.zeros_like(total)
    found[...] = jnp.zeros_like(found)
    pl.semaphore_wait(barrier, n - 1)

    def outgoing(b, u):
        return pltpu.make_async_remote_copy(
            src_ref=sent.at[u, :, part(b)],
            dst_ref=got.at[me, :, part(b)],
            send_sem=send_sem.at[b, u],
            recv_sem=recv_sem.at[b, me],
            device_id=place(rank_of(u, n, groups)),
            device_id_type=MESH,
        )

    def arriving(b, rank):
        return pltpu.make_async_remote_copy(
            src_ref=got.at[rank, :, part(b)],
            dst_ref=got.at[rank, :, part(b)],
            send_sem=send_sem.at[b, 0],
            recv_sem=recv_sem.at[b, rank],
            device_id=place(rank),
            device_id_type=MESH,
        )

    for b in range(phases):
        if b > 0:
            pack(b)

        @pl.when(active)
        def _(b=b):
            own(b).start()

        def start(o, _, b=b):
            u = (mine + o // 2 + o % 2 * ((groups + 1) // 2)) % groups

            @pl.when(rank_of(u, n, groups) != me)
            def _():
                outgoing(b, u).start()

            return 0

        lax.fori_loop(0, groups, start, 0)

    lane = lax.broadcasted_iota(jnp.int32, (SLOTS, LANES), 1)
    zero = jnp.zeros((SLOTS, LANES), jnp.float32)

    def phase(b, _):
        own(b).wait()

        def unpack(half, _):
            for d in range(n_lon):
                rank = d * n_lat + half

                @pl.when(rank != me)
                def _(rank=rank):
                    arriving(b, rank).wait_recv()

                chunk = got[rank, :, part(b)]
                for i in range(group):
                    both[half * group + i, :, d * cols : (d + 1) * cols] = chunk[
                        :, i * cols : (i + 1) * cols
                    ]
            return 0

        lax.fori_loop(0, n_lat, unpack, 0)

        def prepare(i, _):
            w = weights[i // group * rows + b * group + i % group]
            for m in range(tiles):
                at = pl.ds(m * LANES, LANES)
                values = both[i, :, at].astype(jnp.float32)
                fore = values[:SLOTS]
                usable = fore < LIMIT
                fore = jnp.where(usable, fore, 0.0)
                weighted = w * fore
                weight[i, :, at] = jnp.where(usable, w, 0.0)
                fore_w[i, :, at] = weighted
                fore_ww[i, :, at] = weighted * fore
                truth[i, :, at] = values[SLOTS:]
            return 0

        lax.fori_loop(0, n_lat * group, prepare, 0, unroll=2)

        def lag(k, _):
            shift = offsets[k]
            first, turn = lax.div(shift, LANES), lax.rem(shift, LANES)
            stay = lane < LANES - turn
            back_turn = lax.rem(LANES - turn, LANES)
            sums = [(zero, zero, zero)] * tiles
            for i in range(n_lat * group):
                turned = [
                    pltpu.roll(truth[i, :, m * LANES : (m + 1) * LANES], back_turn, 1)
                    for m in range(tiles)
                ]
                ahead = []
                for m in range(tiles):
                    value = turned[m]
                    for f in range(1, tiles):
                        value = jnp.where(first == f, turned[(m + f) % tiles], value)
                    ahead.append(value)
                for m in range(tiles):
                    at = slice(m * LANES, (m + 1) * LANES)
                    true = jnp.where(stay, ahead[m], ahead[(m + 1) % tiles])
                    seen = true < LIMIT
                    true = jnp.where(seen, true, 0.0)
                    cov, var_fore, var_true = sums[m]
                    sums[m] = (
                        cov + fore_w[i, :, at] * true,
                        var_fore + jnp.where(seen, fore_ww[i, :, at], 0.0),
                        var_true + weight[i, :, at] * (true * true),
                    )
            for m in range(tiles):
                at = slice(m * LANES, (m + 1) * LANES)
                for q in range(3):
                    total[k, q, :, at] += sums[m][q]
            return 0

        lax.fori_loop(0, lags, lag, 0)
        return 0

    def returning(rank):
        return pltpu.make_async_remote_copy(
            src_ref=found.at[rank],
            dst_ref=back.at[mine],
            send_sem=result_sem.at[rank],
            recv_sem=back_sem.at[mine],
            device_id=place(rank),
            device_id_type=MESH,
        )

    def returned(u):
        return pltpu.make_async_remote_copy(
            src_ref=back.at[u],
            dst_ref=back.at[u],
            send_sem=result_sem.at[0],
            recv_sem=back_sem.at[u],
            device_id=place(rank_of(u, n, groups)),
            device_id_type=MESH,
        )

    last = pltpu.make_async_copy(found.at[me], back.at[mine], last_sem)

    @pl.when(active)
    def _():
        lax.fori_loop(0, phases, phase, 0)
        for k in range(lags):
            cov, var_fore, var_true = total[k, 0], total[k, 1], total[k, 2]
            value = cov / jnp.sqrt((var_fore + regular_term) * (var_true + regular_term))
            owner, at = k // per_owner, k % per_owner
            for d in range(n_lon):
                found[d * n_lat + owner, :, at * cols : (at + 1) * cols] = value[
                    :, d * cols : (d + 1) * cols
                ]

        def send_back(o, _):
            returning((me + o) % n).start()
            return 0

        lax.fori_loop(1, n, send_back, 0)
        last.start()

        def sent_back(o, _):
            returning((me + o) % n).wait_send()
            return 0

        lax.fori_loop(1, n, sent_back, 0)

    def finish(u, _):
        @pl.when(rank_of(u, n, groups) != me)
        def _():
            for b in range(phases):
                outgoing(b, u).wait_send()
            returned(u).wait_recv()

        return 0

    lax.fori_loop(0, groups, finish, 0)

    @pl.when(active)
    def _():
        last.wait()

    correlation = back[...].reshape(groups * SLOTS, LANES).T
    out[...] = correlation[: per_owner * cols, :channels]


def by_channel(n_lat, n_lon, prediction, observed_state, mean_state, usable_point_flags, offsets):
    rows, cols, channels = prediction.shape
    lags = offsets.shape[0]
    n = n_lat * n_lon
    groups = -(-channels // SLOTS)
    points = rows * cols
    total_rows, total_cols = rows * n_lat, cols * n_lon
    row_index = jnp.arange(total_rows, dtype=jnp.int32).astype(jnp.float32)
    weights = jnp.cos(jnp.pi * ((row_index + 0.5) / total_rows - 0.5))
    group = math.lcm(cols, LANES) // cols
    phases = rows // group
    held = (n_lat * group, SLOTS, total_cols)
    mine = lags // n_lat
    found = pl.pallas_call(
        functools.partial(lag_kernel, (n_lat, n_lon, rows, cols, lags, groups)),
        out_shape=jax.ShapeDtypeStruct((mine * cols, channels), jnp.float32),
        in_specs=[
            pl.BlockSpec(memory_space=pltpu.SMEM),
            pl.BlockSpec(memory_space=pltpu.SMEM),
            pl.BlockSpec(memory_space=pltpu.VMEM),
            pl.BlockSpec(memory_space=pltpu.HBM),
            pl.BlockSpec(memory_space=pltpu.HBM),
            pl.BlockSpec(memory_space=pltpu.HBM),
        ],
        out_specs=pl.BlockSpec(memory_space=pltpu.VMEM),
        scratch_shapes=[
            pltpu.VMEM((3, rows, cols, channels), jnp.bfloat16),
            pltpu.VMEM((groups, 2 * SLOTS, points), jnp.bfloat16),
            pltpu.VMEM((groups, SLOTS, LANES), jnp.float32),
            pltpu.VMEM((n, 2 * SLOTS, points), jnp.bfloat16),
            pltpu.VMEM((n_lat * group, 2 * SLOTS, total_cols), jnp.bfloat16),
            pltpu.VMEM(held, jnp.float32),
            pltpu.VMEM(held, jnp.float32),
            pltpu.VMEM(held, jnp.float32),
            pltpu.VMEM(held, jnp.float32),
            pltpu.VMEM((lags, 3, SLOTS, total_cols), jnp.float32),
            pltpu.VMEM((n, SLOTS, LANES), jnp.float32),
            pltpu.SemaphoreType.DMA((3, phases)),
            pltpu.SemaphoreType.DMA((phases, groups)),
            pltpu.SemaphoreType.DMA((phases, n)),
            pltpu.SemaphoreType.DMA((phases,)),
            pltpu.SemaphoreType.DMA((n,)),
            pltpu.SemaphoreType.DMA((groups,)),
            pltpu.SemaphoreType.DMA,
        ],
        compiler_params=pltpu.CompilerParams(
            collective_id=0, has_side_effects=True, vmem_limit_bytes=40 * 2**20
        ),
    )(offsets, weights, usable_point_flags.T, prediction, observed_state, mean_state)
    return found.reshape(mine, cols, channels)


def fits(n_lat, n_lon, rows, cols, channels, lags):
    n = n_lat * n_lon
    group = math.lcm(cols, LANES) // cols
    return (
        -(-channels // SLOTS) <= n <= channels
        and cols % SLOTS == 0
        and rows % group == 0
        and (cols * n_lon) % LANES == 0
        and lags % n_lat == 0
        and lags // n_lat * cols <= LANES
    )


REACH = 14


def from_behind(value, axis, by):
    count = lax.axis_size(axis)
    return lax.ppermute(value, axis, [(i, (i + by) % count) for i in range(count)])


def ring(prediction, observed_state, mean_state, usable_point_flags, eastward_offsets):
    meridian_extent, parallel_extent, field_total = prediction.shape
    total_rows = meridian_extent * lax.axis_size("lat")
    row_index = (
        lax.axis_index("lat") * meridian_extent + jnp.arange(meridian_extent, dtype=jnp.int32)
    ).astype(jnp.float32)
    weights = jnp.cos(jnp.pi * ((row_index + 0.5) / total_rows - 0.5))
    predicted_mean_state = mean_state.astype(jnp.float32)
    prediction_departure = prediction.astype(jnp.float32) - predicted_mean_state
    observed_departure = (observed_state.astype(jnp.float32) - predicted_mean_state).astype(
        jnp.bfloat16
    )
    base_weight = weights[:, None] * usable_point_flags.astype(jnp.float32)
    window_cols = (REACH + 1) * parallel_extent
    start_true = jnp.zeros((meridian_extent, window_cols, field_total), jnp.bfloat16)
    start_true = lax.dynamic_update_slice_in_dim(start_true, observed_departure, 0, 1)
    start_valid = jnp.zeros((meridian_extent, window_cols), jnp.int32)
    start_valid = lax.dynamic_update_slice_in_dim(start_valid, usable_point_flags, 0, 1)

    def advance(turn_index, state_tuple):
        buffer_true, buffer_valid, slab_true, slab_valid = state_tuple
        slab_true, slab_valid = from_behind((slab_true, slab_valid), "lon", -1)
        place = (turn_index + 1) * parallel_extent
        buffer_true = lax.dynamic_update_slice_in_dim(buffer_true, slab_true, place, 1)
        buffer_valid = lax.dynamic_update_slice_in_dim(buffer_valid, slab_valid, place, 1)
        return (buffer_true, buffer_valid, slab_true, slab_valid)

    win_true, win_valid, unused_true, unused_valid = lax.fori_loop(
        0, REACH, advance, (start_true, start_valid, observed_departure, usable_point_flags)
    )

    def lag_sums(offset):
        frame_segment = lax.dynamic_slice_in_dim(win_true, offset, parallel_extent, 1).astype(
            jnp.float32
        )
        piece_valid = lax.dynamic_slice_in_dim(win_valid, offset, parallel_extent, 1).astype(
            jnp.float32
        )
        couple_factor = (base_weight * piece_valid)[:, :, None]
        joint_moment = jnp.sum(couple_factor * prediction_departure * frame_segment, axis=0)
        prediction_spread = jnp.sum(
            couple_factor * prediction_departure * prediction_departure, axis=0
        )
        var_true = jnp.sum(couple_factor * frame_segment * frame_segment, axis=0)
        return (joint_moment, prediction_spread, var_true)

    joint_moment, prediction_spread, var_true = lax.map(lag_sums, eastward_offsets)
    joint_moment, prediction_spread, var_true = (
        lax.psum_scatter(joint_moment, "lat", scatter_dimension=0, tiled=True),
        lax.psum_scatter(prediction_spread, "lat", scatter_dimension=0, tiled=True),
        lax.psum_scatter(var_true, "lat", scatter_dimension=0, tiled=True),
    )
    return joint_moment / jnp.sqrt((prediction_spread + regular_term) * (var_true + regular_term))


def solution(mesh):
    n_lat, n_lon = mesh.shape["lat"], mesh.shape["lon"]
    placed = (
        P("lat", "lon", None),
        P("lat", "lon", None),
        P("lat", "lon", None),
        P("lat", "lon"),
        P(),
    )

    def local(*args):
        if fits(n_lat, n_lon, *args[0].shape, args[4].shape[0]):
            return by_channel(n_lat, n_lon, *args)
        return ring(*args)

    return jax.shard_map(
        local, mesh=mesh, in_specs=placed, out_specs=P("lat", "lon", None), check_vma=False
    )
```

```python
import functools
import math

import jax
import jax.numpy as jnp
from jax import lax
from jax.experimental import pallas as pl
from jax.experimental.pallas import tpu as pltpu
from jax.sharding import PartitionSpec as P

MESH = pl.DeviceIdType.MESH
LANES = 128
SLOTS = 8
UNUSABLE = 1024.0
LIMIT = 512.0
regular_term = 0.001


def rank_of(u, n, groups):
    return ((u + 1) * n + groups - 1) // groups - 1


def ring_roll(tiles, by, lane):
    count = len(tiles)
    whole, part = by % (count * LANES) // LANES, by % LANES
    tiles = [tiles[(m - whole) % count] for m in range(count)]
    if part == 0:
        return tiles
    turned = [pltpu.roll(x, part, 1) for x in tiles]
    return [jnp.where(lane >= part, turned[m], turned[m - 1]) for m in range(count)]


def lag_kernel(sizes, offsets, weights, flags, prediction, observed, mean, out,
               fields, sent, back, got, fore_w, fore_ww, weight, truth, total, found,
               load_sem, send_sem, recv_sem, own_sem, result_sem, back_sem, last_sem):
    n_lat, n_lon, rows, cols, lags, groups = sizes
    n = n_lat * n_lon
    tiles = n_lon * cols // LANES
    group = math.lcm(cols, LANES) // cols
    phases = rows // group
    width = group * cols
    per_owner = lags // n_lat
    me = lax.axis_index("lon") * n_lat + lax.axis_index("lat")
    mine = me * groups // n
    active = (me + 1) * groups // n > mine

    def place(rank):
        return {"lat": rank % n_lat, "lon": rank // n_lat}

    def part(b):
        return pl.ds(pl.multiple_of(b * width, LANES), width)

    barrier = pltpu.get_barrier_semaphore()

    def greet(o, _):
        pl.semaphore_signal(barrier, inc=1, device_id=place((me + o) % n), device_id_type=MESH)
        return 0

    lax.fori_loop(1, n, greet, 0)

    def load(b):
        at = pl.ds(b * group, group)
        return [
            pltpu.make_async_copy(source.at[at], fields.at[q, at], load_sem.at[q, b])
            for q, source in enumerate((prediction, observed, mean))
        ]

    for b in range(phases):
        for copy in load(b):
            copy.start()

    channels = prediction.shape[2]
    identity = jnp.where(
        lax.broadcasted_iota(jnp.int32, (groups * SLOTS, channels), 0)
        == lax.broadcasted_iota(jnp.int32, (groups * SLOTS, channels), 1),
        1.0,
        0.0,
    ).astype(jnp.bfloat16)

    def pack(b):
        for copy in load(b):
            copy.wait()
        fore, true = [], []
        for i in range(b * group, (b + 1) * group):
            usable = jnp.broadcast_to(flags[:, i : i + 1], (cols, channels)) != 0
            middle = fields[2, i].astype(jnp.float32)
            fore.append(jnp.where(usable, fields[0, i].astype(jnp.float32) - middle, UNUSABLE))
            true.append(jnp.where(usable, fields[1, i].astype(jnp.float32) - middle, UNUSABLE))
        turned = [
            lax.dot_general(
                identity,
                jnp.concatenate(values, axis=0).astype(jnp.bfloat16),
                (((1,), (1,)), ((), ())),
                preferred_element_type=jnp.float32,
            ).reshape(groups, SLOTS, width)
            for values in (fore, true)
        ]
        sent[:, :, b * width : (b + 1) * width] = jnp.concatenate(turned, axis=1).astype(
            jnp.bfloat16
        )

    def own(b):
        return pltpu.make_async_copy(
            sent.at[mine, :, part(b)], got.at[me, :, part(b)], own_sem.at[b]
        )

    pack(0)
    total[...] = jnp.zeros_like(total)
    found[...] = jnp.zeros_like(found)
    pl.semaphore_wait(barrier, n - 1)

    def outgoing(b, u):
        return pltpu.make_async_remote_copy(
            src_ref=sent.at[u, :, part(b)],
            dst_ref=got.at[me, :, part(b)],
            send_sem=send_sem.at[b, u],
            recv_sem=recv_sem.at[b, me],
            device_id=place(rank_of(u, n, groups)),
            device_id_type=MESH,
        )

    def arriving(b, rank):
        return pltpu.make_async_remote_copy(
            src_ref=got.at[rank, :, part(b)],
            dst_ref=got.at[rank, :, part(b)],
            send_sem=send_sem.at[b, 0],
            recv_sem=recv_sem.at[b, rank],
            device_id=place(rank),
            device_id_type=MESH,
        )

    for b in range(phases):
        if b > 0:
            pack(b)

        @pl.when(active)
        def _(b=b):
            own(b).start()

        def start(o, _, b=b):
            u = (mine + o // 2 + o % 2 * ((groups + 1) // 2)) % groups

            @pl.when(rank_of(u, n, groups) != me)
            def _():
                outgoing(b, u).start()

            return 0

        lax.fori_loop(0, groups, start, 0)

    lane = lax.broadcasted_iota(jnp.int32, (SLOTS, LANES), 1)
    zero = jnp.zeros((SLOTS, LANES), jnp.float32)

    def phase(b, _):
        def arrive(o, _):
            arriving(b, (me + o) % n).wait_recv()
            return 0

        own(b).wait()
        lax.fori_loop(1, n, arrive, 0)

        def unpack(half, _):
            chunks = [
                [
                    got[
                        d * n_lat + half,
                        :,
                        pl.ds(pl.multiple_of(b * width + m * LANES, LANES), LANES),
                    ].astype(jnp.float32)
                    for m in range(tiles)
                ]
                for d in range(n_lon)
            ]
            for half_rows, target in ((slice(0, SLOTS), fore_w), (slice(SLOTS, None), truth)):
                skewed = [
                    ring_roll([x[half_rows] for x in chunks[d]], d * cols, lane)
                    for d in range(n_lon)
                ]
                for i in range(group):
                    picked = []
                    for m in range(tiles):
                        place_of = range(m * LANES // cols, -(-(m + 1) * LANES // cols))
                        value = skewed[(place_of[0] - i) % group][m]
                        for p in place_of[1:]:
                            value = jnp.where(
                                lane >= p * cols - m * LANES, skewed[(p - i) % group][m], value
                            )
                        picked.append(value)
                    for m, value in enumerate(ring_roll(picked, -i * cols, lane)):
                        target[half * group + i, :, m * LANES : (m + 1) * LANES] = value
            return 0

        lax.fori_loop(0, n_lat, unpack, 0)

        def prepare(i, _):
            w = weights[i // group * rows + b * group + i % group]
            for m in range(tiles):
                at = pl.ds(m * LANES, LANES)
                fore = fore_w[i, :, at]
                usable = fore < LIMIT
                fore = jnp.where(usable, fore, 0.0)
                weighted = w * fore
                weight[i, :, at] = jnp.where(usable, w, 0.0)
                fore_w[i, :, at] = weighted
                fore_ww[i, :, at] = weighted * fore
            return 0

        lax.fori_loop(0, n_lat * group, prepare, 0, unroll=2)

        def lag(k, _):
            shift = offsets[k]
            first, turn = lax.div(shift, LANES), lax.rem(shift, LANES)
            stay = lane < LANES - turn
            back_turn = lax.rem(LANES - turn, LANES)
            sums = [(zero, zero, zero)] * tiles
            for i in range(n_lat * group):
                turned = [
                    pltpu.roll(truth[i, :, m * LANES : (m + 1) * LANES], back_turn, 1)
                    for m in range(tiles)
                ]
                ahead = []
                for m in range(tiles):
                    value = turned[m]
                    for f in range(1, tiles):
                        value = jnp.where(first == f, turned[(m + f) % tiles], value)
                    ahead.append(value)
                for m in range(tiles):
                    at = slice(m * LANES, (m + 1) * LANES)
                    true = jnp.where(stay, ahead[m], ahead[(m + 1) % tiles])
                    seen = true < LIMIT
                    true = jnp.where(seen, true, 0.0)
                    cov, var_fore, var_true = sums[m]
                    sums[m] = (
                        cov + fore_w[i, :, at] * true,
                        var_fore + jnp.where(seen, fore_ww[i, :, at], 0.0),
                        var_true + weight[i, :, at] * (true * true),
                    )
            for m in range(tiles):
                at = slice(m * LANES, (m + 1) * LANES)
                for q in range(3):
                    total[k, q, :, at] += sums[m][q]
            return 0

        lax.fori_loop(0, lags, lag, 0)
        return 0

    def returning(rank):
        return pltpu.make_async_remote_copy(
            src_ref=found.at[rank],
            dst_ref=back.at[mine],
            send_sem=result_sem.at[rank],
            recv_sem=back_sem.at[mine],
            device_id=place(rank),
            device_id_type=MESH,
        )

    def returned(u):
        return pltpu.make_async_remote_copy(
            src_ref=back.at[u],
            dst_ref=back.at[u],
            send_sem=result_sem.at[0],
            recv_sem=back_sem.at[u],
            device_id=place(rank_of(u, n, groups)),
            device_id_type=MESH,
        )

    last = pltpu.make_async_copy(found.at[me], back.at[mine], last_sem)

    @pl.when(active)
    def _():
        lax.fori_loop(0, phases, phase, 0)
        for k in range(lags):
            cov, var_fore, var_true = total[k, 0], total[k, 1], total[k, 2]
            value = cov / jnp.sqrt((var_fore + regular_term) * (var_true + regular_term))
            owner, at = k // per_owner, k % per_owner
            for d in range(n_lon):
                found[d * n_lat + owner, :, at * cols : (at + 1) * cols] = value[
                    :, d * cols : (d + 1) * cols
                ]

        def send_back(o, _):
            returning((me + o) % n).start()
            return 0

        lax.fori_loop(1, n, send_back, 0)
        last.start()

        def sent_back(o, _):
            returning((me + o) % n).wait_send()
            return 0

        lax.fori_loop(1, n, sent_back, 0)

    def finish(u, _):
        @pl.when(rank_of(u, n, groups) != me)
        def _():
            for b in range(phases):
                outgoing(b, u).wait_send()
            returned(u).wait_recv()

        return 0

    lax.fori_loop(0, groups, finish, 0)

    @pl.when(active)
    def _():
        last.wait()

    correlation = back[...].reshape(groups * SLOTS, LANES).T
    out[...] = correlation[: per_owner * cols, :channels]


def by_channel(n_lat, n_lon, prediction, observed_state, mean_state, usable_point_flags, offsets):
    rows, cols, channels = prediction.shape
    lags = offsets.shape[0]
    n = n_lat * n_lon
    groups = -(-channels // SLOTS)
    points = rows * cols
    total_rows, total_cols = rows * n_lat, cols * n_lon
    row_index = jnp.arange(total_rows, dtype=jnp.int32).astype(jnp.float32)
    weights = jnp.cos(jnp.pi * ((row_index + 0.5) / total_rows - 0.5))
    group = math.lcm(cols, LANES) // cols
    phases = rows // group
    held = (n_lat * group, SLOTS, total_cols)
    mine = lags // n_lat
    found = pl.pallas_call(
        functools.partial(lag_kernel, (n_lat, n_lon, rows, cols, lags, groups)),
        out_shape=jax.ShapeDtypeStruct((mine * cols, channels), jnp.float32),
        in_specs=[
            pl.BlockSpec(memory_space=pltpu.SMEM),
            pl.BlockSpec(memory_space=pltpu.SMEM),
            pl.BlockSpec(memory_space=pltpu.VMEM),
            pl.BlockSpec(memory_space=pltpu.HBM),
            pl.BlockSpec(memory_space=pltpu.HBM),
            pl.BlockSpec(memory_space=pltpu.HBM),
        ],
        out_specs=pl.BlockSpec(memory_space=pltpu.VMEM),
        scratch_shapes=[
            pltpu.VMEM((3, rows, cols, channels), jnp.bfloat16),
            pltpu.VMEM((groups, 2 * SLOTS, points), jnp.bfloat16),
            pltpu.VMEM((groups, SLOTS, LANES), jnp.float32),
            pltpu.VMEM((n, 2 * SLOTS, points), jnp.bfloat16),
            pltpu.VMEM(held, jnp.float32),
            pltpu.VMEM(held, jnp.float32),
            pltpu.VMEM(held, jnp.float32),
            pltpu.VMEM(held, jnp.float32),
            pltpu.VMEM((lags, 3, SLOTS, total_cols), jnp.float32),
            pltpu.VMEM((n, SLOTS, LANES), jnp.float32),
            pltpu.SemaphoreType.DMA((3, phases)),
            pltpu.SemaphoreType.DMA((phases, groups)),
            pltpu.SemaphoreType.DMA((phases, n)),
            pltpu.SemaphoreType.DMA((phases,)),
            pltpu.SemaphoreType.DMA((n,)),
            pltpu.SemaphoreType.DMA((groups,)),
            pltpu.SemaphoreType.DMA,
        ],
        compiler_params=pltpu.CompilerParams(
            collective_id=0, has_side_effects=True, vmem_limit_bytes=40 * 2**20
        ),
    )(offsets, weights, usable_point_flags.T, prediction, observed_state, mean_state)
    return found.reshape(mine, cols, channels)


def fits(n_lat, n_lon, rows, cols, channels, lags):
    n = n_lat * n_lon
    group = math.lcm(cols, LANES) // cols
    return (
        -(-channels // SLOTS) <= n <= channels
        and cols % SLOTS == 0
        and rows % group == 0
        and n_lon == group
        and (cols * n_lon) % LANES == 0
        and lags % n_lat == 0
        and lags // n_lat * cols <= LANES
    )


REACH = 14


def from_behind(value, axis, by):
    count = lax.axis_size(axis)
    return lax.ppermute(value, axis, [(i, (i + by) % count) for i in range(count)])


def ring(prediction, observed_state, mean_state, usable_point_flags, eastward_offsets):
    meridian_extent, parallel_extent, field_total = prediction.shape
    total_rows = meridian_extent * lax.axis_size("lat")
    row_index = (
        lax.axis_index("lat") * meridian_extent + jnp.arange(meridian_extent, dtype=jnp.int32)
    ).astype(jnp.float32)
    weights = jnp.cos(jnp.pi * ((row_index + 0.5) / total_rows - 0.5))
    predicted_mean_state = mean_state.astype(jnp.float32)
    prediction_departure = prediction.astype(jnp.float32) - predicted_mean_state
    observed_departure = (observed_state.astype(jnp.float32) - predicted_mean_state).astype(
        jnp.bfloat16
    )
    base_weight = weights[:, None] * usable_point_flags.astype(jnp.float32)
    window_cols = (REACH + 1) * parallel_extent
    start_true = jnp.zeros((meridian_extent, window_cols, field_total), jnp.bfloat16)
    start_true = lax.dynamic_update_slice_in_dim(start_true, observed_departure, 0, 1)
    start_valid = jnp.zeros((meridian_extent, window_cols), jnp.int32)
    start_valid = lax.dynamic_update_slice_in_dim(start_valid, usable_point_flags, 0, 1)

    def advance(turn_index, state_tuple):
        buffer_true, buffer_valid, slab_true, slab_valid = state_tuple
        slab_true, slab_valid = from_behind((slab_true, slab_valid), "lon", -1)
        place = (turn_index + 1) * parallel_extent
        buffer_true = lax.dynamic_update_slice_in_dim(buffer_true, slab_true, place, 1)
        buffer_valid = lax.dynamic_update_slice_in_dim(buffer_valid, slab_valid, place, 1)
        return (buffer_true, buffer_valid, slab_true, slab_valid)

    win_true, win_valid, unused_true, unused_valid = lax.fori_loop(
        0, REACH, advance, (start_true, start_valid, observed_departure, usable_point_flags)
    )

    def lag_sums(offset):
        frame_segment = lax.dynamic_slice_in_dim(win_true, offset, parallel_extent, 1).astype(
            jnp.float32
        )
        piece_valid = lax.dynamic_slice_in_dim(win_valid, offset, parallel_extent, 1).astype(
            jnp.float32
        )
        couple_factor = (base_weight * piece_valid)[:, :, None]
        joint_moment = jnp.sum(couple_factor * prediction_departure * frame_segment, axis=0)
        prediction_spread = jnp.sum(
            couple_factor * prediction_departure * prediction_departure, axis=0
        )
        var_true = jnp.sum(couple_factor * frame_segment * frame_segment, axis=0)
        return (joint_moment, prediction_spread, var_true)

    joint_moment, prediction_spread, var_true = lax.map(lag_sums, eastward_offsets)
    joint_moment, prediction_spread, var_true = (
        lax.psum_scatter(joint_moment, "lat", scatter_dimension=0, tiled=True),
        lax.psum_scatter(prediction_spread, "lat", scatter_dimension=0, tiled=True),
        lax.psum_scatter(var_true, "lat", scatter_dimension=0, tiled=True),
    )
    return joint_moment / jnp.sqrt((prediction_spread + regular_term) * (var_true + regular_term))


def solution(mesh):
    n_lat, n_lon = mesh.shape["lat"], mesh.shape["lon"]
    placed = (
        P("lat", "lon", None),
        P("lat", "lon", None),
        P("lat", "lon", None),
        P("lat", "lon"),
        P(),
    )

    def local(*args):
        if fits(n_lat, n_lon, *args[0].shape, args[4].shape[0]):
            return by_channel(n_lat, n_lon, *args)
        return ring(*args)

    return jax.shard_map(
        local, mesh=mesh, in_specs=placed, out_specs=P("lat", "lon", None), check_vma=False
    )
```

```python
import functools
import math

import jax
import jax.numpy as jnp
import numpy as np
from jax import lax
from jax.experimental import pallas as pl
from jax.experimental.pallas import tpu as pltpu
from jax.sharding import PartitionSpec as P

MESH = pl.DeviceIdType.MESH
LANES = 128
SLOTS = 8
UNUSABLE = 1024.0
LIMIT = 512.0
regular_term = 0.001


def rank_of(u, n, groups):
    return ((u + 1) * n + groups - 1) // groups - 1


def ring_roll(tiles, by, lane):
    count = len(tiles)
    whole, part = by % (count * LANES) // LANES, by % LANES
    tiles = [tiles[(m - whole) % count] for m in range(count)]
    if part == 0:
        return tiles
    turned = [pltpu.roll(x, part, 1) for x in tiles]
    return [jnp.where(lane >= part, turned[m], turned[m - 1]) for m in range(count)]


def lag_kernel(sizes, offsets, weights, flags, prediction, observed, mean, out,
               fields, sent, back, got, fore_w, fore_ww, weight, truth, total, found,
               load_sem, send_sem, recv_sem, own_sem, result_sem, back_sem, last_sem):
    n_lat, n_lon, rows, cols, lags, groups = sizes
    n = n_lat * n_lon
    tiles = n_lon * cols // LANES
    group = math.lcm(cols, LANES) // cols
    phases = rows // group
    width = group * cols
    per_owner = lags // n_lat
    me = lax.axis_index("lon") * n_lat + lax.axis_index("lat")
    mine = me * groups // n
    active = (me + 1) * groups // n > mine

    def place(rank):
        return {"lat": rank % n_lat, "lon": rank // n_lat}

    barrier = pltpu.get_barrier_semaphore()

    def greet(o, _):
        pl.semaphore_signal(barrier, inc=1, device_id=place((me + o) % n), device_id_type=MESH)
        return 0

    lax.fori_loop(1, n, greet, 0)

    def load(b):
        at = pl.ds(b * group, group)
        return [
            pltpu.make_async_copy(source.at[at], fields.at[q, at], load_sem.at[q, b])
            for q, source in enumerate((prediction, observed, mean))
        ]

    for b in range(phases):
        for copy in load(b):
            copy.start()

    channels = prediction.shape[2]
    identity = jnp.where(
        lax.broadcasted_iota(jnp.int32, (groups * SLOTS, channels), 0)
        == lax.broadcasted_iota(jnp.int32, (groups * SLOTS, channels), 1),
        1.0,
        0.0,
    ).astype(jnp.bfloat16)

    def pack(b):
        for copy in load(b):
            copy.wait()
        fore, true = [], []
        for i in range(b * group, (b + 1) * group):
            usable = jnp.broadcast_to(flags[:, i : i + 1], (cols, channels)) != 0
            middle = fields[2, i].astype(jnp.float32)
            fore.append(jnp.where(usable, fields[0, i].astype(jnp.float32) - middle, UNUSABLE))
            true.append(jnp.where(usable, fields[1, i].astype(jnp.float32) - middle, UNUSABLE))
        turned = [
            lax.dot_general(
                identity,
                jnp.concatenate(values, axis=0).astype(jnp.bfloat16),
                (((1,), (1,)), ((), ())),
                preferred_element_type=jnp.float32,
            ).reshape(groups, SLOTS, width)
            for values in (fore, true)
        ]
        sent[b] = jnp.concatenate(turned, axis=1).astype(
            jnp.bfloat16
        )

    def own(b):
        return pltpu.make_async_copy(
            sent.at[b, mine], got.at[b, me], own_sem.at[b]
        )

    pack(0)
    total[...] = jnp.zeros_like(total)
    found[...] = jnp.zeros_like(found)
    pl.semaphore_wait(barrier, n - 1)

    def outgoing(b, u):
        return pltpu.make_async_remote_copy(
            src_ref=sent.at[b, u],
            dst_ref=got.at[b, me],
            send_sem=send_sem.at[b, u],
            recv_sem=recv_sem.at[b, me],
            device_id=place(rank_of(u, n, groups)),
            device_id_type=MESH,
        )

    def arriving(b, rank):
        return pltpu.make_async_remote_copy(
            src_ref=got.at[b, rank],
            dst_ref=got.at[b, rank],
            send_sem=send_sem.at[b, 0],
            recv_sem=recv_sem.at[b, rank],
            device_id=place(rank),
            device_id_type=MESH,
        )

    for b in range(phases):
        if b > 0:
            pack(b)

        @pl.when(active)
        def _(b=b):
            own(b).start()

        def start(o, _, b=b):
            u = (mine + o // 2 + o % 2 * ((groups + 1) // 2)) % groups

            @pl.when(rank_of(u, n, groups) != me)
            def _():
                outgoing(b, u).start()

            return 0

        lax.fori_loop(0, groups, start, 0)

    lane = lax.broadcasted_iota(jnp.int32, (SLOTS, LANES), 1)
    zero = jnp.zeros((SLOTS, LANES), jnp.float32)

    def phase(b, _):
        def arrive(o, _):
            arriving(b, (me + o) % n).wait_recv()
            return 0

        own(b).wait()
        lax.fori_loop(1, n, arrive, 0)

        def unpack(half, _):
            chunks = [
                [
                    got[b, d * n_lat + half, :, m * LANES : (m + 1) * LANES].astype(jnp.float32)
                    for m in range(tiles)
                ]
                for d in range(n_lon)
            ]
            for half_rows, target in ((slice(0, SLOTS), fore_w), (slice(SLOTS, None), truth)):
                skewed = [
                    ring_roll([x[half_rows] for x in chunks[d]], d * cols, lane)
                    for d in range(n_lon)
                ]
                for i in range(group):
                    picked = []
                    for m in range(tiles):
                        place_of = range(m * LANES // cols, -(-(m + 1) * LANES // cols))
                        value = skewed[(place_of[0] - i) % group][m]
                        for p in place_of[1:]:
                            value = jnp.where(
                                lane >= p * cols - m * LANES, skewed[(p - i) % group][m], value
                            )
                        picked.append(value)
                    for m, value in enumerate(ring_roll(picked, -i * cols, lane)):
                        target[half * group + i, :, m * LANES : (m + 1) * LANES] = value
            return 0

        lax.fori_loop(0, n_lat, unpack, 0)

        def prepare(i, _):
            w = weights[i // group * rows + b * group + i % group]
            for m in range(tiles):
                at = pl.ds(m * LANES, LANES)
                fore = fore_w[i, :, at]
                usable = fore < LIMIT
                fore = jnp.where(usable, fore, 0.0)
                weighted = w * fore
                weight[i, :, at] = jnp.where(usable, w, 0.0)
                fore_w[i, :, at] = weighted
                fore_ww[i, :, at] = weighted * fore
            return 0

        lax.fori_loop(0, n_lat * group, prepare, 0, unroll=2)

        def lag(k, _):
            shift = offsets[k]
            first, turn = lax.div(shift, LANES), lax.rem(shift, LANES)
            stay = lane < LANES - turn
            back_turn = lax.rem(LANES - turn, LANES)
            sums = [(zero, zero, zero)] * tiles
            for i in range(n_lat * group):
                turned = [
                    pltpu.roll(truth[i, :, m * LANES : (m + 1) * LANES], back_turn, 1)
                    for m in range(tiles)
                ]
                ahead = []
                for m in range(tiles):
                    value = turned[m]
                    for f in range(1, tiles):
                        value = jnp.where(first == f, turned[(m + f) % tiles], value)
                    ahead.append(value)
                for m in range(tiles):
                    at = slice(m * LANES, (m + 1) * LANES)
                    true = jnp.where(stay, ahead[m], ahead[(m + 1) % tiles])
                    seen = true < LIMIT
                    true = jnp.where(seen, true, 0.0)
                    cov, var_fore, var_true = sums[m]
                    sums[m] = (
                        cov + fore_w[i, :, at] * true,
                        var_fore + jnp.where(seen, fore_ww[i, :, at], 0.0),
                        var_true + weight[i, :, at] * (true * true),
                    )
            for m in range(tiles):
                at = slice(m * LANES, (m + 1) * LANES)
                for q in range(3):
                    total[k, q, :, at] += sums[m][q]
            return 0

        lax.fori_loop(0, lags, lag, 0)
        return 0

    def returning(rank):
        return pltpu.make_async_remote_copy(
            src_ref=found.at[rank],
            dst_ref=back.at[mine],
            send_sem=result_sem.at[rank],
            recv_sem=back_sem.at[mine],
            device_id=place(rank),
            device_id_type=MESH,
        )

    def returned(u):
        return pltpu.make_async_remote_copy(
            src_ref=back.at[u],
            dst_ref=back.at[u],
            send_sem=result_sem.at[0],
            recv_sem=back_sem.at[u],
            device_id=place(rank_of(u, n, groups)),
            device_id_type=MESH,
        )

    last = pltpu.make_async_copy(found.at[me], back.at[mine], last_sem)

    @pl.when(active)
    def _():
        lax.fori_loop(0, phases, phase, 0)
        for k in range(lags):
            cov, var_fore, var_true = total[k, 0], total[k, 1], total[k, 2]
            value = cov / jnp.sqrt((var_fore + regular_term) * (var_true + regular_term))
            owner, at = k // per_owner, k % per_owner
            for d in range(n_lon):
                found[d * n_lat + owner, :, at * cols : (at + 1) * cols] = value[
                    :, d * cols : (d + 1) * cols
                ]

        def send_back(o, _):
            returning((me + o) % n).start()
            return 0

        lax.fori_loop(1, n, send_back, 0)
        last.start()

        def sent_back(o, _):
            returning((me + o) % n).wait_send()
            return 0

        lax.fori_loop(1, n, sent_back, 0)

    def finish(u, _):
        @pl.when(rank_of(u, n, groups) != me)
        def _():
            for b in range(phases):
                outgoing(b, u).wait_send()
            returned(u).wait_recv()

        return 0

    lax.fori_loop(0, groups, finish, 0)

    @pl.when(active)
    def _():
        last.wait()

    correlation = back[...].reshape(groups * SLOTS, LANES).T
    out[...] = correlation[: per_owner * cols, :channels]


def by_channel(n_lat, n_lon, prediction, observed_state, mean_state, usable_point_flags, offsets):
    rows, cols, channels = prediction.shape
    lags = offsets.shape[0]
    n = n_lat * n_lon
    groups = -(-channels // SLOTS)
    total_rows, total_cols = rows * n_lat, cols * n_lon
    latitude = np.pi * ((np.arange(total_rows) + 0.5) / total_rows - 0.5)
    weights = jnp.asarray(np.cos(latitude), jnp.float32)
    group = math.lcm(cols, LANES) // cols
    phases = rows // group
    held = (n_lat * group, SLOTS, total_cols)
    mine = lags // n_lat
    found = pl.pallas_call(
        functools.partial(lag_kernel, (n_lat, n_lon, rows, cols, lags, groups)),
        out_shape=jax.ShapeDtypeStruct((mine * cols, channels), jnp.float32),
        in_specs=[
            pl.BlockSpec(memory_space=pltpu.SMEM),
            pl.BlockSpec(memory_space=pltpu.SMEM),
            pl.BlockSpec(memory_space=pltpu.VMEM),
            pl.BlockSpec(memory_space=pltpu.HBM),
            pl.BlockSpec(memory_space=pltpu.HBM),
            pl.BlockSpec(memory_space=pltpu.HBM),
        ],
        out_specs=pl.BlockSpec(memory_space=pltpu.VMEM),
        scratch_shapes=[
            pltpu.VMEM((3, rows, cols, channels), jnp.bfloat16),
            pltpu.VMEM((phases, groups, 2 * SLOTS, group * cols), jnp.bfloat16),
            pltpu.VMEM((groups, SLOTS, LANES), jnp.float32),
            pltpu.VMEM((phases, n, 2 * SLOTS, group * cols), jnp.bfloat16),
            pltpu.VMEM(held, jnp.float32),
            pltpu.VMEM(held, jnp.float32),
            pltpu.VMEM(held, jnp.float32),
            pltpu.VMEM(held, jnp.float32),
            pltpu.VMEM((lags, 3, SLOTS, total_cols), jnp.float32),
            pltpu.VMEM((n, SLOTS, LANES), jnp.float32),
            pltpu.SemaphoreType.DMA((3, phases)),
            pltpu.SemaphoreType.DMA((phases, groups)),
            pltpu.SemaphoreType.DMA((phases, n)),
            pltpu.SemaphoreType.DMA((phases,)),
            pltpu.SemaphoreType.DMA((n,)),
            pltpu.SemaphoreType.DMA((groups,)),
            pltpu.SemaphoreType.DMA,
        ],
        compiler_params=pltpu.CompilerParams(
            collective_id=0, has_side_effects=True, vmem_limit_bytes=60 * 2**20
        ),
    )(offsets, weights, usable_point_flags.T, prediction, observed_state, mean_state)
    return found.reshape(mine, cols, channels)


def fits(n_lat, n_lon, rows, cols, channels, lags):
    n = n_lat * n_lon
    group = math.lcm(cols, LANES) // cols
    return (
        -(-channels // SLOTS) <= n <= channels
        and cols % SLOTS == 0
        and rows % group == 0
        and n_lon == group
        and (cols * n_lon) % LANES == 0
        and lags % n_lat == 0
        and lags // n_lat * cols <= LANES
    )


REACH = 14


def from_behind(value, axis, by):
    count = lax.axis_size(axis)
    return lax.ppermute(value, axis, [(i, (i + by) % count) for i in range(count)])


def ring(prediction, observed_state, mean_state, usable_point_flags, eastward_offsets):
    meridian_extent, parallel_extent, field_total = prediction.shape
    total_rows = meridian_extent * lax.axis_size("lat")
    row_index = (
        lax.axis_index("lat") * meridian_extent + jnp.arange(meridian_extent, dtype=jnp.int32)
    ).astype(jnp.float32)
    weights = jnp.cos(jnp.pi * ((row_index + 0.5) / total_rows - 0.5))
    predicted_mean_state = mean_state.astype(jnp.float32)
    prediction_departure = prediction.astype(jnp.float32) - predicted_mean_state
    observed_departure = (observed_state.astype(jnp.float32) - predicted_mean_state).astype(
        jnp.bfloat16
    )
    base_weight = weights[:, None] * usable_point_flags.astype(jnp.float32)
    window_cols = (REACH + 1) * parallel_extent
    start_true = jnp.zeros((meridian_extent, window_cols, field_total), jnp.bfloat16)
    start_true = lax.dynamic_update_slice_in_dim(start_true, observed_departure, 0, 1)
    start_valid = jnp.zeros((meridian_extent, window_cols), jnp.int32)
    start_valid = lax.dynamic_update_slice_in_dim(start_valid, usable_point_flags, 0, 1)

    def advance(turn_index, state_tuple):
        buffer_true, buffer_valid, slab_true, slab_valid = state_tuple
        slab_true, slab_valid = from_behind((slab_true, slab_valid), "lon", -1)
        place = (turn_index + 1) * parallel_extent
        buffer_true = lax.dynamic_update_slice_in_dim(buffer_true, slab_true, place, 1)
        buffer_valid = lax.dynamic_update_slice_in_dim(buffer_valid, slab_valid, place, 1)
        return (buffer_true, buffer_valid, slab_true, slab_valid)

    win_true, win_valid, unused_true, unused_valid = lax.fori_loop(
        0, REACH, advance, (start_true, start_valid, observed_departure, usable_point_flags)
    )

    def lag_sums(offset):
        frame_segment = lax.dynamic_slice_in_dim(win_true, offset, parallel_extent, 1).astype(
            jnp.float32
        )
        piece_valid = lax.dynamic_slice_in_dim(win_valid, offset, parallel_extent, 1).astype(
            jnp.float32
        )
        couple_factor = (base_weight * piece_valid)[:, :, None]
        joint_moment = jnp.sum(couple_factor * prediction_departure * frame_segment, axis=0)
        prediction_spread = jnp.sum(
            couple_factor * prediction_departure * prediction_departure, axis=0
        )
        var_true = jnp.sum(couple_factor * frame_segment * frame_segment, axis=0)
        return (joint_moment, prediction_spread, var_true)

    joint_moment, prediction_spread, var_true = lax.map(lag_sums, eastward_offsets)
    joint_moment, prediction_spread, var_true = (
        lax.psum_scatter(joint_moment, "lat", scatter_dimension=0, tiled=True),
        lax.psum_scatter(prediction_spread, "lat", scatter_dimension=0, tiled=True),
        lax.psum_scatter(var_true, "lat", scatter_dimension=0, tiled=True),
    )
    return joint_moment / jnp.sqrt((prediction_spread + regular_term) * (var_true + regular_term))


def solution(mesh):
    n_lat, n_lon = mesh.shape["lat"], mesh.shape["lon"]
    placed = (
        P("lat", "lon", None),
        P("lat", "lon", None),
        P("lat", "lon", None),
        P("lat", "lon"),
        P(),
    )

    def local(*args):
        if fits(n_lat, n_lon, *args[0].shape, args[4].shape[0]):
            return by_channel(n_lat, n_lon, *args)
        return ring(*args)

    return jax.shard_map(
        local, mesh=mesh, in_specs=placed, out_specs=P("lat", "lon", None), check_vma=False
    )
```

```python
import functools
import math

import jax
import jax.numpy as jnp
import numpy as np
from jax import lax
from jax.experimental import pallas as pl
from jax.experimental.pallas import tpu as pltpu
from jax.sharding import PartitionSpec as P

MESH = pl.DeviceIdType.MESH
LANES = 128
SLOTS = 8
UNUSABLE = 1024.0
LIMIT = 512.0
regular_term = 0.001


def rank_of(u, n, groups):
    return ((u + 1) * n + groups - 1) // groups - 1


def lag_kernel(sizes, offsets, weights, flags, prediction, observed, mean, out,
               fields, sent, back, got, fore_w, fore_ww, weight, truth, total, found,
               load_sem, send_sem, recv_sem, own_sem, result_sem, back_sem, last_sem):
    n_lat, n_lon, rows, cols, lags, groups = sizes
    n = n_lat * n_lon
    tiles = n_lon * cols // LANES
    group = math.lcm(cols, LANES) // cols
    phases = rows // group
    width = group * cols
    per_owner = lags // n_lat
    me = lax.axis_index("lon") * n_lat + lax.axis_index("lat")
    mine = me * groups // n
    active = (me + 1) * groups // n > mine

    def place(rank):
        return {"lat": rank % n_lat, "lon": rank // n_lat}

    def part(b):
        return pl.ds(pl.multiple_of(b * width, LANES), width)

    barrier = pltpu.get_barrier_semaphore()

    def greet(o, _):
        pl.semaphore_signal(barrier, inc=1, device_id=place((me + o) % n), device_id_type=MESH)
        return 0

    lax.fori_loop(1, n, greet, 0)

    def load(b):
        at = pl.ds(b * group, group)
        return [
            pltpu.make_async_copy(source.at[at], fields.at[q, at], load_sem.at[q, b])
            for q, source in enumerate((prediction, observed, mean))
        ]

    for b in range(phases):
        for copy in load(b):
            copy.start()

    channels = prediction.shape[2]
    identity = jnp.where(
        lax.broadcasted_iota(jnp.int32, (groups * SLOTS, channels), 0)
        == lax.broadcasted_iota(jnp.int32, (groups * SLOTS, channels), 1),
        1.0,
        0.0,
    ).astype(jnp.bfloat16)

    def pack(b):
        for copy in load(b):
            copy.wait()
        fore, true = [], []
        for i in range(b * group, (b + 1) * group):
            usable = jnp.broadcast_to(flags[:, i : i + 1], (cols, channels)) != 0
            middle = fields[2, i].astype(jnp.float32)
            fore.append(jnp.where(usable, fields[0, i].astype(jnp.float32) - middle, UNUSABLE))
            true.append(jnp.where(usable, fields[1, i].astype(jnp.float32) - middle, UNUSABLE))
        turned = [
            lax.dot_general(
                identity,
                jnp.concatenate(values, axis=0).astype(jnp.bfloat16),
                (((1,), (1,)), ((), ())),
                preferred_element_type=jnp.float32,
            ).reshape(groups, SLOTS, width)
            for values in (fore, true)
        ]
        sent[:, :, b * width : (b + 1) * width] = jnp.concatenate(turned, axis=1).astype(
            jnp.bfloat16
        )

    def own(b):
        return pltpu.make_async_copy(
            sent.at[mine, :, part(b)], got.at[me, :, part(b)], own_sem.at[b]
        )

    pack(0)
    total[...] = jnp.zeros_like(total)
    found[...] = jnp.zeros_like(found)
    pl.semaphore_wait(barrier, n - 1)

    def outgoing(b, u):
        return pltpu.make_async_remote_copy(
            src_ref=sent.at[u, :, part(b)],
            dst_ref=got.at[me, :, part(b)],
            send_sem=send_sem.at[b, u],
            recv_sem=recv_sem.at[b, me],
            device_id=place(rank_of(u, n, groups)),
            device_id_type=MESH,
        )

    def arriving(b, rank):
        return pltpu.make_async_remote_copy(
            src_ref=got.at[rank, :, part(b)],
            dst_ref=got.at[rank, :, part(b)],
            send_sem=send_sem.at[b, 0],
            recv_sem=recv_sem.at[b, rank],
            device_id=place(rank),
            device_id_type=MESH,
        )

    for b in range(phases):
        if b > 0:
            pack(b)

        @pl.when(active)
        def _(b=b):
            own(b).start()

        def start(o, _, b=b):
            u = (mine + o // 2 + o % 2 * ((groups + 1) // 2)) % groups

            @pl.when(rank_of(u, n, groups) != me)
            def _():
                outgoing(b, u).start()

            return 0

        lax.fori_loop(0, groups, start, 0)

    lane = lax.broadcasted_iota(jnp.int32, (SLOTS, LANES), 1)
    zero = jnp.zeros((SLOTS, LANES), jnp.float32)

    def phase(b, _):
        def arrive(o, _):
            arriving(b, (me + o) % n).wait_recv()
            return 0

        own(b).wait()
        lax.fori_loop(1, n, arrive, 0)

        def unpack(half, _):
            for d in range(n_lon):
                chunk = got[d * n_lat + half, :, part(b)].astype(jnp.float32)
                for i in range(group):
                    piece = chunk[:, i * cols : (i + 1) * cols]
                    fore_w[half * group + i, :, d * cols : (d + 1) * cols] = piece[:SLOTS]
                    truth[half * group + i, :, d * cols : (d + 1) * cols] = piece[SLOTS:]
            return 0

        lax.fori_loop(0, n_lat, unpack, 0)

        def prepare(i, _):
            w = weights[i // group * rows + b * group + i % group]
            for m in range(tiles):
                at = pl.ds(m * LANES, LANES)
                fore = fore_w[i, :, at]
                usable = fore < LIMIT
                fore = jnp.where(usable, fore, 0.0)
                weighted = w * fore
                weight[i, :, at] = jnp.where(usable, w, 0.0)
                fore_w[i, :, at] = weighted
                fore_ww[i, :, at] = weighted * fore
            return 0

        lax.fori_loop(0, n_lat * group, prepare, 0, unroll=2)

        def lag(k, _):
            shift = offsets[k]
            first, turn = lax.div(shift, LANES), lax.rem(shift, LANES)
            stay = lane < LANES - turn
            back_turn = lax.rem(LANES - turn, LANES)
            sums = [(zero, zero, zero)] * tiles
            for i in range(n_lat * group):
                turned = [
                    pltpu.roll(truth[i, :, m * LANES : (m + 1) * LANES], back_turn, 1)
                    for m in range(tiles)
                ]
                ahead = []
                for m in range(tiles):
                    value = turned[m]
                    for f in range(1, tiles):
                        value = jnp.where(first == f, turned[(m + f) % tiles], value)
                    ahead.append(value)
                for m in range(tiles):
                    at = slice(m * LANES, (m + 1) * LANES)
                    true = jnp.where(stay, ahead[m], ahead[(m + 1) % tiles])
                    seen = true < LIMIT
                    true = jnp.where(seen, true, 0.0)
                    cov, var_fore, var_true = sums[m]
                    sums[m] = (
                        cov + fore_w[i, :, at] * true,
                        var_fore + jnp.where(seen, fore_ww[i, :, at], 0.0),
                        var_true + weight[i, :, at] * (true * true),
                    )
            for m in range(tiles):
                at = slice(m * LANES, (m + 1) * LANES)
                for q in range(3):
                    total[k, q, :, at] += sums[m][q]
            return 0

        lax.fori_loop(0, lags, lag, 0)
        return 0

    def returning(rank):
        return pltpu.make_async_remote_copy(
            src_ref=found.at[rank],
            dst_ref=back.at[mine],
            send_sem=result_sem.at[rank],
            recv_sem=back_sem.at[mine],
            device_id=place(rank),
            device_id_type=MESH,
        )

    def returned(u):
        return pltpu.make_async_remote_copy(
            src_ref=back.at[u],
            dst_ref=back.at[u],
            send_sem=result_sem.at[0],
            recv_sem=back_sem.at[u],
            device_id=place(rank_of(u, n, groups)),
            device_id_type=MESH,
        )

    last = pltpu.make_async_copy(found.at[me], back.at[mine], last_sem)

    @pl.when(active)
    def _():
        lax.fori_loop(0, phases, phase, 0)
        for k in range(lags):
            cov, var_fore, var_true = total[k, 0], total[k, 1], total[k, 2]
            value = cov / jnp.sqrt((var_fore + regular_term) * (var_true + regular_term))
            owner, at = k // per_owner, k % per_owner
            for d in range(n_lon):
                found[d * n_lat + owner, :, at * cols : (at + 1) * cols] = value[
                    :, d * cols : (d + 1) * cols
                ]
            if at == per_owner - 1:

                def send_back(d, _, owner=owner):
                    @pl.when(d * n_lat + owner != me)
                    def _():
                        returning(d * n_lat + owner).start()

                    return 0

                lax.fori_loop(0, n_lon, send_back, 0)

        last.start()

        def sent_back(o, _):
            returning((me + o) % n).wait_send()
            return 0

        lax.fori_loop(1, n, sent_back, 0)

    def finish(u, _):
        @pl.when(rank_of(u, n, groups) != me)
        def _():
            for b in range(phases):
                outgoing(b, u).wait_send()
            returned(u).wait_recv()

        return 0

    lax.fori_loop(0, groups, finish, 0)

    @pl.when(active)
    def _():
        last.wait()

    correlation = back[...].reshape(groups * SLOTS, LANES).T
    out[...] = correlation[: per_owner * cols, :channels]


def by_channel(n_lat, n_lon, prediction, observed_state, mean_state, usable_point_flags, offsets):
    rows, cols, channels = prediction.shape
    lags = offsets.shape[0]
    n = n_lat * n_lon
    groups = -(-channels // SLOTS)
    points = rows * cols
    total_rows, total_cols = rows * n_lat, cols * n_lon
    latitude = np.pi * ((np.arange(total_rows) + 0.5) / total_rows - 0.5)
    weights = jnp.asarray(np.cos(latitude), jnp.float32)
    group = math.lcm(cols, LANES) // cols
    phases = rows // group
    held = (n_lat * group, SLOTS, total_cols)
    mine = lags // n_lat
    found = pl.pallas_call(
        functools.partial(lag_kernel, (n_lat, n_lon, rows, cols, lags, groups)),
        out_shape=jax.ShapeDtypeStruct((mine * cols, channels), jnp.float32),
        in_specs=[
            pl.BlockSpec(memory_space=pltpu.SMEM),
            pl.BlockSpec(memory_space=pltpu.SMEM),
            pl.BlockSpec(memory_space=pltpu.VMEM),
            pl.BlockSpec(memory_space=pl.ANY),
            pl.BlockSpec(memory_space=pl.ANY),
            pl.BlockSpec(memory_space=pl.ANY),
        ],
        out_specs=pl.BlockSpec(memory_space=pltpu.VMEM),
        scratch_shapes=[
            pltpu.VMEM((3, rows, cols, channels), jnp.bfloat16),
            pltpu.VMEM((groups, 2 * SLOTS, points), jnp.bfloat16),
            pltpu.VMEM((groups, SLOTS, LANES), jnp.float32),
            pltpu.VMEM((n, 2 * SLOTS, points), jnp.bfloat16),
            pltpu.VMEM(held, jnp.float32),
            pltpu.VMEM(held, jnp.float32),
            pltpu.VMEM(held, jnp.float32),
            pltpu.VMEM(held, jnp.float32),
            pltpu.VMEM((lags, 3, SLOTS, total_cols), jnp.float32),
            pltpu.VMEM((n, SLOTS, LANES), jnp.float32),
            pltpu.SemaphoreType.DMA((3, phases)),
            pltpu.SemaphoreType.DMA((phases, groups)),
            pltpu.SemaphoreType.DMA((phases, n)),
            pltpu.SemaphoreType.DMA((phases,)),
            pltpu.SemaphoreType.DMA((n,)),
            pltpu.SemaphoreType.DMA((groups,)),
            pltpu.SemaphoreType.DMA,
        ],
        compiler_params=pltpu.CompilerParams(
            collective_id=0, has_side_effects=True, vmem_limit_bytes=60 * 2**20
        ),
    )(offsets, weights, usable_point_flags.T, prediction, observed_state, mean_state)
    return found.reshape(mine, cols, channels)


def fits(n_lat, n_lon, rows, cols, channels, lags):
    n = n_lat * n_lon
    group = math.lcm(cols, LANES) // cols
    return (
        -(-channels // SLOTS) <= n <= channels
        and cols % SLOTS == 0
        and rows % group == 0
        and (cols * n_lon) % LANES == 0
        and lags % n_lat == 0
        and lags // n_lat * cols <= LANES
    )


REACH = 14


def from_behind(value, axis, by):
    count = lax.axis_size(axis)
    return lax.ppermute(value, axis, [(i, (i + by) % count) for i in range(count)])


def ring(prediction, observed_state, mean_state, usable_point_flags, eastward_offsets):
    meridian_extent, parallel_extent, field_total = prediction.shape
    total_rows = meridian_extent * lax.axis_size("lat")
    row_index = (
        lax.axis_index("lat") * meridian_extent + jnp.arange(meridian_extent, dtype=jnp.int32)
    ).astype(jnp.float32)
    weights = jnp.cos(jnp.pi * ((row_index + 0.5) / total_rows - 0.5))
    predicted_mean_state = mean_state.astype(jnp.float32)
    prediction_departure = prediction.astype(jnp.float32) - predicted_mean_state
    observed_departure = (observed_state.astype(jnp.float32) - predicted_mean_state).astype(
        jnp.bfloat16
    )
    base_weight = weights[:, None] * usable_point_flags.astype(jnp.float32)
    window_cols = (REACH + 1) * parallel_extent
    start_true = jnp.zeros((meridian_extent, window_cols, field_total), jnp.bfloat16)
    start_true = lax.dynamic_update_slice_in_dim(start_true, observed_departure, 0, 1)
    start_valid = jnp.zeros((meridian_extent, window_cols), jnp.int32)
    start_valid = lax.dynamic_update_slice_in_dim(start_valid, usable_point_flags, 0, 1)

    def advance(turn_index, state_tuple):
        buffer_true, buffer_valid, slab_true, slab_valid = state_tuple
        slab_true, slab_valid = from_behind((slab_true, slab_valid), "lon", -1)
        place = (turn_index + 1) * parallel_extent
        buffer_true = lax.dynamic_update_slice_in_dim(buffer_true, slab_true, place, 1)
        buffer_valid = lax.dynamic_update_slice_in_dim(buffer_valid, slab_valid, place, 1)
        return (buffer_true, buffer_valid, slab_true, slab_valid)

    win_true, win_valid, unused_true, unused_valid = lax.fori_loop(
        0, REACH, advance, (start_true, start_valid, observed_departure, usable_point_flags)
    )

    def lag_sums(offset):
        frame_segment = lax.dynamic_slice_in_dim(win_true, offset, parallel_extent, 1).astype(
            jnp.float32
        )
        piece_valid = lax.dynamic_slice_in_dim(win_valid, offset, parallel_extent, 1).astype(
            jnp.float32
        )
        couple_factor = (base_weight * piece_valid)[:, :, None]
        joint_moment = jnp.sum(couple_factor * prediction_departure * frame_segment, axis=0)
        prediction_spread = jnp.sum(
            couple_factor * prediction_departure * prediction_departure, axis=0
        )
        var_true = jnp.sum(couple_factor * frame_segment * frame_segment, axis=0)
        return (joint_moment, prediction_spread, var_true)

    joint_moment, prediction_spread, var_true = lax.map(lag_sums, eastward_offsets)
    joint_moment, prediction_spread, var_true = (
        lax.psum_scatter(joint_moment, "lat", scatter_dimension=0, tiled=True),
        lax.psum_scatter(prediction_spread, "lat", scatter_dimension=0, tiled=True),
        lax.psum_scatter(var_true, "lat", scatter_dimension=0, tiled=True),
    )
    return joint_moment / jnp.sqrt((prediction_spread + regular_term) * (var_true + regular_term))


def solution(mesh):
    n_lat, n_lon = mesh.shape["lat"], mesh.shape["lon"]
    placed = (
        P("lat", "lon", None),
        P("lat", "lon", None),
        P("lat", "lon", None),
        P("lat", "lon"),
        P(),
    )

    def local(*args):
        if fits(n_lat, n_lon, *args[0].shape, args[4].shape[0]):
            return by_channel(n_lat, n_lon, *args)
        return ring(*args)

    return jax.shard_map(
        local, mesh=mesh, in_specs=placed, out_specs=P("lat", "lon", None), check_vma=False
    )
```
